128 devices in a mesh: row: 16 (over z_hi, y, core), col: 8 (over x, z_lo).
Axes of the slice: x: 4, y: 4, z: 4 (z_hi: 2, z_lo: 2; z = z_hi * 2 + z_lo), core: 2. Of those that a mesh axis runs over, the one named last changes fastest.
Arguments:
- image_tokens: bfloat16 [1, 256, 128, 1024], P(None, 'row', 'col'), may hold values from -6 to 6
- qkv_three: bfloat16 [3, 1024, 1024], replicated, may hold values from -0.125 to 0.125, as said below
- proj_three: bfloat16 [1024, 1024], replicated, may hold values from -0.1875 to 0.1875
- scale_three: float32 [32], replicated, may hold values from 1.6 to 5
- table_three: float32 [961, 32], replicated, may hold values from -6 to 6
- gain_three: float32 [1024], replicated, may hold values from 0.25 to 1.75
- merge_weight: bfloat16 [4096, 2048], P(None, 'row'), may hold values from -0.09375 to 0.09375
- merge_gain: float32 [2048], replicated, may hold values from 0.25 to 1.75
- qkv_four: bfloat16 [3, 2048, 2048], P(None, None, 'row'), may hold values from -0.088388348 to 0.088388348, as said below
- proj_four: bfloat16 [2048, 2048], P('row'), may hold values from -0.125 to 0.125
- scale_four: float32 [64], P('row'), may hold values from 1.6 to 5
- table_four: float32 [961, 64], P(None, 'row'), may hold values from -6 to 6
- gain_attend: float32 [2048], replicated, may hold values from 0.25 to 1.75
- expand_weight: bfloat16 [2048, 8192], P(None, 'row'), may hold values from -0.125 to 0.125
- reduce_weight: bfloat16 [8192, 2048], P('row'), may hold values from -0.0625 to 0.0625
- gain_feed: float32 [2048], replicated, may hold values from 0.25 to 1.75
Outputs:
- section_out: bfloat16 [1, 128, 64, 2048], P(None, 'row', 'col')
The draws below stay inside these ranges and needn't reach their ends.
Inputs may be any that keep to these rules, and one draw needn't show every extreme that they name: `qkv_three`: a projection's entries, about 1024 ** -0.5 in deviation. `qkv_four`: a projection's entries, about 2048 ** -0.5 in deviation.
All inputs are finite; a program needn't handle non-finite values.
Results may differ from the reference program's by a relative error of at most 0.035.
The reference program's roundings to bfloat16 on the way count: a program that leaves them out, or rounds other values in their place, can miss the bound.
Values may be sent and summed in bfloat16 or wider, within the bound.
No kernel may reach another device: no remote copies, remote signals or barrier semaphores. Data moves between devices by JAX's collectives and lax.ppermute only.
A program may use at most 192 MiB of HBM per device.

```python
import math
import jax
import jax.numpy as jnp
from jax import lax

C3 = 1024
HD = 32
HEADS3 = 32
C4 = 2048
HEADS4 = 64
FF4 = 8192
WIN = 16
IMAGES = 1
H3 = 256
W3 = 128
OFFSETS = 961


def draw_qkv_three(key, part):
    key = jax.random.fold_in(key, 11)
    base = jnp.clip(jax.random.normal(key, (3, C3, C3), jnp.float32), -4.0, 4.0) * C3 ** (-0.5)
    return base.astype(jnp.bfloat16)


def draw_qkv_four(key, part):
    key = jax.random.fold_in(key, 23)
    base = jnp.clip(jax.random.normal(key, (3, C4, C4), jnp.float32), -4.0, 4.0) * C4 ** (-0.5)
    return base.astype(jnp.bfloat16)


def block_scale(stream_key, shape, cuts, low, largest):
    level = 1.0
    for dim, shards_of in cuts:
        draws = jax.random.uniform(jax.random.fold_in(jax.random.fold_in(stream_key, 6), dim), (shards_of,), jnp.float32, low / len(cuts), largest / len(cuts))
        level = level * jnp.repeat(jnp.exp(draws), shape[dim] // shards_of).reshape((-1,) + (1,) * (len(shape) - 1 - dim))
    return level


def centred(rng, extent, scale, limit, cuts=(), kind=jnp.bfloat16):
    entries = jax.random.normal(rng, extent, jnp.float32) * scale
    if len(cuts) > 0:
        entries = block_scale(rng, extent, cuts, -0.22, 0.18) * entries
    return jnp.clip(entries, min=-limit, max=limit).astype(kind)


def setup_inputs(seed: int = 0) -> dict:
    streams_of = jax.random.split(jax.random.key(seed), 17)
    return {
        "image_tokens": centred(streams_of[0], (IMAGES, H3, W3, C3), 1.0, 6.0, ((1, 16), (2, 8))),
        "qkv_three": draw_qkv_three(jax.random.fold_in(streams_of[16], 71), 0),
        "proj_three": centred(streams_of[2], (C3, C3), C3 ** -0.5, 0.1875),
        "scale_three": jnp.clip(jax.random.uniform(streams_of[3], (HEADS3,), jnp.float32, 1.6, 5.0), 1.6, 5.0),
        "table_three": centred(streams_of[4], (OFFSETS, HEADS3), 1.5, 6.0, (), jnp.float32),
        "gain_three": jnp.clip(1.0 + 0.15 * jax.random.normal(streams_of[5], (C3,), jnp.float32), 0.25, 1.75),
        "merge_weight": centred(streams_of[6], (4 * C3, C4), (4 * C3) ** -0.5, 0.09375, ((1, 16),)),
        "merge_gain": jnp.clip(1.0 + 0.15 * jax.random.normal(streams_of[7], (C4,), jnp.float32), 0.25, 1.75),
        "qkv_four": draw_qkv_four(jax.random.fold_in(streams_of[16], 71), 0),
        "proj_four": centred(streams_of[9], (C4, C4), C4 ** -0.5, 0.125, ((0, 16),)),
        "scale_four": jnp.clip(1.6 + 3.4 * jax.random.uniform(streams_of[10], (HEADS4,), jnp.float32) ** block_scale(streams_of[10], (HEADS4,), ((0, 16),), -0.2, 0.2), 1.6, 5.0),
        "table_four": centred(streams_of[11], (OFFSETS, HEADS4), 1.5, 6.0, ((1, 16),), jnp.float32),
        "gain_attend": jnp.clip(1.0 + 0.15 * jax.random.normal(streams_of[12], (C4,), jnp.float32), 0.25, 1.75),
        "expand_weight": centred(streams_of[13], (C4, FF4), C4 ** -0.5, 0.125, ((1, 16),)),
        "reduce_weight": centred(streams_of[14], (FF4, C4), FF4 ** -0.5, 0.0625, ((0, 16),)),
        "gain_feed": jnp.clip(1.0 + 0.15 * jax.random.normal(streams_of[15], (C4,), jnp.float32), 0.25, 1.75),
    }


EPSILON = 1e-05
FLOOR = 1e-06

def relative_index(window):
    coords = jnp.arange(window * window, dtype=jnp.int32)
    rows_at = coords // window
    cols_at = coords % window
    spread = (rows_at[:, None] - rows_at[None, :] + window - 1) * (2 * window - 1)
    return (spread + cols_at[:, None] - cols_at[None, :] + window - 1).astype(jnp.int32)

def position_bias(table, window):
    looked = jnp.take(table, relative_index(window), axis=0)
    return jnp.transpose(16.0 * jax.nn.sigmoid(looked), (2, 0, 1))

def layer_norm(values, gain):
    centre = values - lax.optimization_barrier(jnp.mean(values, axis=-1, keepdims=True))
    spread = lax.optimization_barrier(jnp.mean(centre * centre, axis=-1, keepdims=True))
    return centre * lax.rsqrt(spread + EPSILON) * gain

def unit_rows(values):
    length = jnp.sqrt(lax.optimization_barrier(jnp.sum(values * values, axis=-1, keepdims=True)))
    return (values / jnp.maximum(length, FLOOR)).astype(jnp.bfloat16)

def attend(queries, keys_all, values_all, logit, pos_bias, region_mask):
    query_unit = lax.optimization_barrier(unit_rows(queries.astype(jnp.float32))).astype(jnp.float32)
    key_unit = lax.optimization_barrier(unit_rows(keys_all.astype(jnp.float32))).astype(jnp.float32)
    scaled = jnp.exp(jnp.minimum(logit, math.log(100.0)))
    scores = jnp.einsum('nqhd,nkhd->nhqk', query_unit, key_unit) * scaled[None, :, None, None]
    scores = scores + pos_bias[None] + region_mask[:, None]
    peak = lax.optimization_barrier(jnp.max(scores, axis=-1, keepdims=True))
    weights = jnp.exp(scores - peak)
    probs = lax.optimization_barrier((weights / lax.optimization_barrier(jnp.sum(weights, axis=-1, keepdims=True))).astype(jnp.bfloat16))
    return jnp.einsum('nhqk,nkhd->nqhd', probs.astype(jnp.float32), values_all.astype(jnp.float32))

def windows(tensor, window):
    batch, height, width = tensor.shape[:3]
    rest = tensor.shape[3:]
    shaped = tensor.reshape((batch, height // window, window, width // window, window) + rest)
    shaped = jnp.moveaxis(shaped, 3, 2)
    return shaped.reshape((batch * (height // window) * (width // window), window * window) + rest)

def unwindows(tensor, batch, height, width, window):
    rest = tensor.shape[2:]
    shaped = tensor.reshape((batch, height // window, width // window, window, window) + rest)
    shaped = jnp.moveaxis(shaped, 2, 3)
    return shaped.reshape((batch, height, width) + rest)

def window_map(queries, keys_all, values_all, logit, pos_bias, region_mask):

    def single(item):
        return attend(item[0][None], item[1][None], item[2][None], logit, pos_bias, item[3][None])[0]
    return lax.map(single, (queries, keys_all, values_all, region_mask))

def reference(image_tokens, qkv_three, proj_three, scale_three, table_three, gain_three, merge_weight, merge_gain, qkv_four, proj_four, scale_four, table_four, gain_attend, expand_weight, reduce_weight, gain_feed):
    batch, height, width, chans = image_tokens.shape
    half_win = WIN // 2
    rolled = jnp.roll(image_tokens, (-half_win, -half_win), (1, 2))
    projected = jnp.einsum('bhwc,scd->sbhwd', rolled.astype(jnp.float32), qkv_three.astype(jnp.float32)).astype(jnp.bfloat16)
    head_three = chans // HD
    split = projected.reshape(3, batch, height, width, head_three, HD)
    rows_at = jnp.arange(height, dtype=jnp.int32)
    cols_at = jnp.arange(width, dtype=jnp.int32)
    row_label = (rows_at >= height - WIN).astype(jnp.int32) + (rows_at >= height - half_win).astype(jnp.int32)
    col_label = (cols_at >= width - WIN).astype(jnp.int32) + (cols_at >= width - half_win).astype(jnp.int32)
    labels = jnp.broadcast_to((3 * row_label[:, None] + col_label[None, :])[None], (batch, height, width))
    label_win = windows(labels, WIN)
    region_mask = jnp.where(label_win[:, :, None] != label_win[:, None, :], -100.0, 0.0).astype(jnp.float32)
    attended = window_map(windows(split[0], WIN), windows(split[1], WIN), windows(split[2], WIN), scale_three, position_bias(table_three, WIN), region_mask)
    attended = unwindows(attended.reshape(attended.shape[0], WIN * WIN, chans), batch, height, width, WIN).astype(jnp.bfloat16)
    mixed = jnp.dot(attended.reshape(-1, chans), proj_three, preferred_element_type=jnp.float32).reshape(batch, height, width, chans)
    section_three = (rolled.astype(jnp.float32) + layer_norm(mixed, gain_three)).astype(jnp.bfloat16)
    section_three = jnp.roll(section_three, (half_win, half_win), (1, 2))
    grid = section_three.reshape(batch, height // 2, 2, width // 2, 2, chans)
    quadrants = jnp.concatenate([grid[:, :, 0, :, 0], grid[:, :, 1, :, 0], grid[:, :, 0, :, 1], grid[:, :, 1, :, 1]], axis=-1)
    wide = merge_weight.shape[1]
    low_height = height // 2
    low_width = width // 2
    reduced = jnp.dot(quadrants.reshape(-1, 4 * chans), merge_weight, preferred_element_type=jnp.float32)
    merged = layer_norm(reduced, merge_gain).astype(jnp.bfloat16).reshape(batch, low_height, low_width, wide)
    projected_four = jnp.einsum('bhwc,scd->sbhwd', merged.astype(jnp.float32), qkv_four.astype(jnp.float32)).astype(jnp.bfloat16)
    head_four = wide // HD
    split_four = projected_four.reshape(3, batch, low_height, low_width, head_four, HD)
    count = batch * (low_height // WIN) * (low_width // WIN)
    blank = jnp.zeros((count, WIN * WIN, WIN * WIN), jnp.float32)
    attended_four = window_map(windows(split_four[0], WIN), windows(split_four[1], WIN), windows(split_four[2], WIN), scale_four, position_bias(table_four, WIN), blank)
    attended_four = unwindows(attended_four.reshape(count, WIN * WIN, wide), batch, low_height, low_width, WIN).astype(jnp.bfloat16)
    mixed_four = jnp.dot(attended_four.reshape(-1, wide), proj_four, preferred_element_type=jnp.float32).reshape(batch, low_height, low_width, wide)
    after_attend = (merged.astype(jnp.float32) + layer_norm(mixed_four, gain_attend)).astype(jnp.bfloat16)
    hidden = jax.nn.gelu(jnp.dot(after_attend.reshape(-1, wide), expand_weight, preferred_element_type=jnp.float32), approximate=False).astype(jnp.bfloat16)
    feed = jnp.dot(hidden, reduce_weight, preferred_element_type=jnp.float32).reshape(batch, low_height, low_width, wide)
    return (after_attend.astype(jnp.float32) + layer_norm(feed, gain_feed)).astype(jnp.bfloat16)
```

```python
import functools
import math

import jax
import jax.numpy as jnp
from jax import lax
from jax.experimental import pallas as pl
from jax.experimental.pallas import tpu as pltpu
from jax.sharding import PartitionSpec as P

HD = 32
WIN = 16
TOKENS = WIN * WIN
GROUP = 8
TILE = 64
LANES = 128

EPSILON = 1e-05
FLOOR = 1e-06

ROWS = 16
COLS = 8
VMEM = 56 * 1024 * 1024


def place_of(row, col):
    return row // 8, row // 2 % 4, row % 2, col // 2, col % 2


def flat_of(zh, y, core, x, zl):
    return (zh * 8 + y * 2 + core) * COLS + x * 2 + zl


def permute(value, target):
    pairs = [
        (row * COLS + col, target(row, col)) for row in range(ROWS) for col in range(COLS)
    ]
    return lax.ppermute(value, ("row", "col"), pairs)


def home(row, col):
    zh, y, core, x, zl = place_of(row % ROWS, col % COLS)
    return flat_of(zh ^ zl, y // 2 * 2 + core, y % 2, x, zl)


def unhome(row, col):
    zh, y, core, x, zl = place_of(row, col)
    return flat_of(zh ^ zl, y // 2 * 2 + core, y % 2, x, zl)


MEMBERS = tuple((dy, dz) for dy in range(4) for dz in range(2))
BLOCKS = tuple((dy, dz, 0) for dy in range(4) for dz in range(2)) + tuple(
    (dy, dz, 1) for dz in range(2) for dy in range(4)
)


def onward(row, col, dy, dz):
    zh, y, core, x, zl = place_of(row, col)
    return flat_of(zh ^ dz, (y + dy) % 4, core, x, zl ^ dz)


def send(value, dy, dz):
    return permute(value, functools.partial(onward, dy=dy, dz=dz))


def gather(low, high):
    side = send(low, 0, 1)
    near = [high, send(high, 1, 0), None, send(high, 3, 0)]
    near[2] = send(high, 2, 0)
    both = jnp.concatenate([low, side], axis=0)
    lows = [both, send(both, 1, 0), None, send(both, 3, 0)]
    lows[2] = send(both, 2, 0)
    highs = jnp.concatenate(near, axis=0)
    return lows + [highs, send(highs, 0, 1)]


def scatter(parts):
    order = (2, 6, 1, 3, 7, 4, 5)
    got = {i: send(parts[i], *MEMBERS[i]) for i in order}
    return [parts[0]] + [got[i] for i in range(1, GROUP)]


def other_core(value):
    return permute(value, lambda row, col: (row ^ 1) * COLS + col)


def table_rows(table):
    heads = table.shape[1]
    span = 2 * WIN - 1
    grid = jnp.transpose(16.0 * jax.nn.sigmoid(table)).reshape(heads, span, span)
    grid = jnp.pad(grid, ((0, 0), (0, 1), (0, 1))).reshape(heads, 8, 4, 32)
    return jnp.transpose(grid, (0, 2, 1, 3)).reshape(heads, 4, 256)


def build_bias(rows, bias_ref):
    lane = lax.broadcasted_iota(jnp.int32, (WIN, 256), 1)
    slot = lane % 32 // 8
    lows = jnp.zeros((WIN, 256), jnp.float32)
    highs = jnp.zeros((WIN, 256), jnp.float32)
    for r in range(4):
        wide = jnp.broadcast_to(rows[r : r + 1], (WIN, 256))
        skew = pltpu.roll(wide, 256 - 15, 1, stride=1, stride_axis=0)
        low = pltpu.roll(skew, 8 * r, 1) if r else skew
        high = pltpu.roll(skew, (8 * r - 8) % 256, 1) if r != 1 else skew
        lows = jnp.where(slot == r, low, lows)
        highs = jnp.where(slot == r, high, highs)
    for c in range(WIN):
        by = (256 - (15 - c) * 8) % 256
        low = pltpu.roll(lows, by, 1) if by else lows
        high = pltpu.roll(highs, by, 1) if by else highs
        for half in range(2):
            at = (half * WIN + c) * 8
            bias_ref[at : at + 8, 0:LANES] = low[half * 8 : half * 8 + 8, 0:LANES]
            bias_ref[at : at + 8, LANES : 2 * LANES] = high[half * 8 : half * 8 + 8, 0:LANES]


def unit_heads(values):
    down = lax.broadcasted_iota(jnp.int32, (LANES, LANES), 0) // HD
    across = lax.broadcasted_iota(jnp.int32, (LANES, LANES), 1) // HD
    same = (down == across).astype(jnp.float32)
    squares = jnp.dot(
        values * values,
        same,
        precision=lax.Precision.HIGHEST,
        preferred_element_type=jnp.float32,
    )
    return (values / jnp.maximum(jnp.sqrt(squares), FLOOR)).astype(jnp.bfloat16)


def head_attend(queries, keys, values_t, head, scaled, bias, mask):
    lane = lax.broadcasted_iota(jnp.int32, queries.shape, 1) // HD
    own = jnp.where(lane == head, queries, jnp.zeros_like(queries))
    scores = lax.dot_general(
        keys, own, (((1,), (1,)), ((), ())), preferred_element_type=jnp.float32
    )
    scores = scores * scaled + bias
    if mask is not None:
        scores = scores + mask
    peak = jnp.max(scores, axis=0, keepdims=True)
    weights = jnp.exp(scores - peak)
    total = jnp.sum(weights, axis=0, keepdims=True)
    probs = (weights * (1.0 / total)).astype(jnp.bfloat16)
    return jnp.dot(values_t, probs, preferred_element_type=jnp.float32)


def norm(values, gain):
    centre = values - jnp.mean(values, axis=-1, keepdims=True)
    spread = jnp.mean(centre * centre, axis=-1, keepdims=True)
    return centre * lax.rsqrt(spread + EPSILON) * gain


def first_kernel(
    last_ref, scale_ref, x_ref, qkv_ref, rows_ref, proj_ref, gain_ref, *rest
):
    outs, (bias, mask, attended) = rest[:4], rest[4:]
    step = pl.program_id(0)

    @pl.when(step == 0)
    def _():
        down = lax.broadcasted_iota(jnp.int32, (TOKENS, TOKENS), 0) // TILE
        across = lax.broadcasted_iota(jnp.int32, (TOKENS, TOKENS), 1) // TILE
        apart = jnp.where(down % 2 != across % 2, last_ref[0], 0)
        apart = apart + jnp.where(down // 2 != across // 2, last_ref[1], 0)
        mask[...] = jnp.where(apart > 0, -100.0, 0.0).astype(jnp.float32)

    x = x_ref[...]
    q, k, v = (
        jnp.dot(x, qkv_ref[s], preferred_element_type=jnp.float32).astype(jnp.bfloat16)
        for s in range(3)
    )
    q = unit_heads(q.astype(jnp.float32))
    k = unit_heads(k.astype(jnp.float32))
    v = jnp.transpose(v)
    heads = LANES // HD
    for head in range(heads):
        build_bias(rows_ref[head], bias)
        out = head_attend(
            q,
            k,
            v[head * HD : (head + 1) * HD],
            head,
            scale_ref[step * heads + head],
            bias[...],
            mask[...],
        )
        at = pl.multiple_of(step * LANES + head * HD, HD)
        attended[pl.ds(at, HD), :] = out.astype(jnp.bfloat16)

    @pl.when(step == pl.num_programs(0) - 1)
    def _():
        mixed = lax.dot_general(
            attended[...],
            proj_ref[...],
            (((0,), (0,)), ((), ())),
            preferred_element_type=jnp.float32,
        )
        section = (x.astype(jnp.float32) + norm(mixed, gain_ref[...])).astype(jnp.bfloat16)
        at = lax.broadcasted_iota(jnp.int32, (TILE, TILE), 0)
        source = at // 4 % 4 * 16 + at // 16 % 2 * 8 + at % 4 * 2 + at // 32
        pick = (lax.broadcasted_iota(jnp.int32, (TILE, TILE), 1) == source).astype(jnp.bfloat16)
        chans = x.shape[1]
        for quadrant in range(4):
            rows = section[quadrant * TILE : (quadrant + 1) * TILE]
            moved = jnp.dot(pick, rows, preferred_element_type=jnp.float32).astype(jnp.bfloat16)
            for part in range(4):
                outs[quadrant][:, part * chans : (part + 1) * chans] = moved[
                    part * 16 : (part + 1) * 16
                ]


def first_attention(last, scaled, x, qkv, rows, proj, gain):
    chans = x.shape[1]
    smem = pl.BlockSpec(memory_space=pltpu.SMEM)
    heads = LANES // HD
    return pl.pallas_call(
        first_kernel,
        grid=(chans // LANES,),
        in_specs=[
            smem,
            smem,
            pl.BlockSpec((TOKENS, chans), lambda i: (0, 0)),
            pl.BlockSpec((3, chans, LANES), lambda i: (0, 0, i)),
            pl.BlockSpec((heads, 4, 256), lambda i: (i, 0, 0)),
            pl.BlockSpec((chans, chans), lambda i: (0, 0)),
            pl.BlockSpec((1, chans), lambda i: (0, 0)),
        ],
        out_specs=[pl.BlockSpec((16, 4 * chans), lambda i: (0, 0))] * 4,
        out_shape=[jax.ShapeDtypeStruct((16, 4 * chans), jnp.bfloat16)] * 4,
        scratch_shapes=[
            pltpu.VMEM((TOKENS, TOKENS), jnp.float32),
            pltpu.VMEM((TOKENS, TOKENS), jnp.float32),
            pltpu.VMEM((chans, TOKENS), jnp.bfloat16),
        ],
        compiler_params=pltpu.CompilerParams(vmem_limit_bytes=VMEM),
        name="first_attention",
    )(last, scaled, x, qkv, rows, proj, gain)


PIECES = 6


def lay(pieces, whole):
    at = 0
    for piece in pieces:
        rows = piece.shape[0]
        whole[at : at + rows, :] = piece[...]
        at += rows


def merge_kernel(core_ref, *refs):
    pieces, (own_ref, other_ref, low_ref, high_ref, x) = refs[:PIECES], refs[PIECES:]
    lay(pieces, x)
    own = jnp.dot(x[...], own_ref[...], preferred_element_type=jnp.float32).astype(jnp.bfloat16)
    other = jnp.dot(x[...], other_ref[...], preferred_element_type=jnp.float32).astype(jnp.bfloat16)
    first = core_ref[0] == 0
    for half, out_ref in enumerate((low_ref, high_ref)):
        at = slice(half * TOKENS, (half + 1) * TOKENS)
        out_ref[:, 0:LANES] = jnp.where(first, own[at], other[at])
        out_ref[:, LANES : 2 * LANES] = jnp.where(first, other[at], own[at])


def merge(core, pieces, own, other):
    smem = pl.BlockSpec(memory_space=pltpu.SMEM)
    vmem = pl.BlockSpec(memory_space=pltpu.VMEM)
    tokens = GROUP * TILE
    return pl.pallas_call(
        merge_kernel,
        in_specs=[smem] + [vmem] * (PIECES + 2),
        out_specs=[vmem] * 2,
        out_shape=[jax.ShapeDtypeStruct((TOKENS, 2 * LANES), jnp.bfloat16)] * 2,
        scratch_shapes=[pltpu.VMEM((tokens, pieces[0].shape[1]), jnp.bfloat16)],
        compiler_params=pltpu.CompilerParams(vmem_limit_bytes=VMEM),
        name="merge_patches",
    )(core, *pieces, own, other)


def second_kernel(at_ref, scale_ref, *refs):
    parts, refs = refs[:PIECES], refs[PIECES:]
    qkv_refs, rows_refs, proj_refs, gain_ref = refs[0:2], refs[2:4], refs[4:6], refs[6]
    merged_ref, outs = refs[7], refs[8:16]
    merged, bias, attended, sums = refs[16:]
    wide = 2 * LANES
    half = TILE // 2
    whole = GROUP * wide
    for dy, dz, part in BLOCKS:
        row = pl.multiple_of(at_ref[dy * 2 + dz] * TILE + part * half, half)
        pieces = []
        for fy, fz in MEMBERS:
            ty, tz = (dy - fy) % 4, dz ^ fz
            block = BLOCKS.index((ty, tz, part)) % GROUP * half
            if part == 0:
                source, start = parts[fy], fz * TOKENS
            else:
                source, start = parts[4 + fz], fy * TOKENS
            piece = source[start + block : start + block + half, :]
            pieces.append(piece.astype(jnp.float32))
        mean = sum(jnp.sum(piece, axis=-1, keepdims=True) for piece in pieces) / whole
        pieces = [piece - mean for piece in pieces]
        spread = sum(jnp.sum(piece * piece, axis=-1, keepdims=True) for piece in pieces) / whole
        inverse = lax.rsqrt(spread + EPSILON)
        for i, piece in enumerate(pieces):
            col = pl.multiple_of(at_ref[GROUP + i] * wide, wide)
            values = piece * inverse * gain_ref[:, pl.ds(col, wide)]
            merged[pl.ds(row, half), pl.ds(col, wide)] = values.astype(jnp.bfloat16)
    merged_ref[...] = merged[pl.ds(pl.multiple_of(at_ref[0] * TILE, TILE), TILE), :]

    heads = LANES // HD
    for side in range(2):
        x = merged[...]
        q, k, v = (
            jnp.dot(x, qkv_refs[side][s], preferred_element_type=jnp.float32).astype(jnp.bfloat16)
            for s in range(3)
        )
        q = unit_heads(q.astype(jnp.float32))
        k = unit_heads(k.astype(jnp.float32))
        v = jnp.transpose(v)
        for head in range(heads):
            build_bias(rows_refs[side][head], bias)
            for window in range(2):
                at = slice(window * TOKENS, (window + 1) * TOKENS)
                out = head_attend(
                    q[at],
                    k[at],
                    v[head * HD : (head + 1) * HD, at],
                    head,
                    scale_ref[side * heads + head],
                    bias[...],
                    None,
                )
                base = side * LANES + head * HD
                attended[base : base + HD, at] = out.astype(jnp.bfloat16)
    total = None
    for side in range(2):
        part = lax.dot_general(
            attended[side * LANES : (side + 1) * LANES, :],
            proj_refs[side][...],
            (((0,), (0,)), ((), ())),
            preferred_element_type=jnp.float32,
        )
        total = part if total is None else total + part
    sums[...] = total.astype(jnp.bfloat16)
    for i, (dy, dz) in enumerate(MEMBERS):
        place = at_ref[-dy % 4 * 2 + dz]
        outs[i][...] = sums[pl.ds(pl.multiple_of(place * TILE, TILE), TILE), :]


def second_attention(at, scaled, parts, qkv, rows, proj, gain):
    smem = pl.BlockSpec(memory_space=pltpu.SMEM)
    vmem = pl.BlockSpec(memory_space=pltpu.VMEM)
    chans = gain.shape[1]
    tokens = GROUP * TILE
    tile = jax.ShapeDtypeStruct((TILE, chans), jnp.bfloat16)
    return pl.pallas_call(
        second_kernel,
        in_specs=[smem, smem] + [vmem] * (PIECES + 7),
        out_specs=[vmem] * (GROUP + 1),
        out_shape=[tile] * (GROUP + 1),
        scratch_shapes=[
            pltpu.VMEM((tokens, chans), jnp.bfloat16),
            pltpu.VMEM((TOKENS, TOKENS), jnp.float32),
            pltpu.VMEM((2 * LANES, tokens), jnp.bfloat16),
            pltpu.VMEM((tokens, chans), jnp.bfloat16),
        ],
        compiler_params=pltpu.CompilerParams(vmem_limit_bytes=VMEM),
        name="second_attention",
    )(at, scaled, *parts, *qkv, *rows, *proj, gain)


def feed_kernel(*refs):
    pieces, refs = refs[:PIECES], refs[PIECES:]
    expand, reduce, outs, (x, total) = refs[0:2], refs[2:4], refs[4:12], refs[12:]
    step = pl.program_id(0)

    @pl.when(step == 0)
    def _():
        lay(pieces, x)

    part = None
    for side in range(2):
        lifted = jnp.dot(x[...], expand[side][...], preferred_element_type=jnp.float32)
        hidden = (0.5 * lifted * (1.0 + lax.erf(lifted * math.sqrt(0.5)))).astype(jnp.bfloat16)
        more = jnp.dot(hidden, reduce[side][...], preferred_element_type=jnp.float32)
        part = more if part is None else part + more

    @pl.when(step == 0)
    def _():
        total[...] = part

    @pl.when(step != 0)
    def _():
        total[...] = total[...] + part

    @pl.when(step == pl.num_programs(0) - 1)
    def _():
        half = TILE // 2
        for i, (dy, dz) in enumerate(MEMBERS):
            for part in range(2):
                at = BLOCKS.index((-dy % 4, dz, part)) * half
                values = total[at : at + half, :].astype(jnp.bfloat16)
                outs[i][part * half : (part + 1) * half, :] = values


def feed_forward(pieces, expand, reduce):
    chans, units = expand[0].shape
    block = 2 * LANES
    tokens = GROUP * TILE
    whole = pl.BlockSpec((TILE, chans), lambda i: (0, 0))
    return pl.pallas_call(
        feed_kernel,
        grid=(units // block,),
        in_specs=[pl.BlockSpec(piece.shape, lambda i: (0, 0)) for piece in pieces]
        + [pl.BlockSpec((chans, block), lambda i: (0, i))] * 2
        + [pl.BlockSpec((block, chans), lambda i: (i, 0))] * 2,
        out_specs=[whole] * GROUP,
        out_shape=[jax.ShapeDtypeStruct((TILE, chans), jnp.bfloat16)] * GROUP,
        scratch_shapes=[
            pltpu.VMEM((tokens, chans), jnp.bfloat16),
            pltpu.VMEM((tokens, chans), jnp.float32),
        ],
        compiler_params=pltpu.CompilerParams(vmem_limit_bytes=VMEM),
        name="feed_forward",
    )(*pieces, *expand, *reduce)


def join_kernel(*refs):
    parts, (base_ref, gain_ref, out_ref) = refs[:GROUP], refs[GROUP:]
    total = sum(part[...].astype(jnp.float32) for part in parts)
    out_ref[...] = (base_ref[...].astype(jnp.float32) + norm(total, gain_ref[...])).astype(
        jnp.bfloat16
    )


def join(parts, base, gain):
    vmem = pl.BlockSpec(memory_space=pltpu.VMEM)
    return pl.pallas_call(
        join_kernel,
        in_specs=[vmem] * (GROUP + 2),
        out_specs=vmem,
        out_shape=jax.ShapeDtypeStruct(base.shape, jnp.bfloat16),
        compiler_params=pltpu.CompilerParams(vmem_limit_bytes=VMEM),
        name="join_sums",
    )(*parts, base, gain)


def on_device(
    image_tokens,
    qkv_three,
    proj_three,
    scale_three,
    table_three,
    gain_three,
    merge_weight,
    merge_gain,
    qkv_four,
    proj_four,
    scale_four,
    table_four,
    gain_attend,
    expand_weight,
    reduce_weight,
    gain_feed,
):
    chans = image_tokens.shape[3]
    half = WIN // 2
    row = lax.axis_index("row")
    col = lax.axis_index("col")
    zh, y, core, zl = row // 8, row // 2 % 4, row % 2, col % 2
    limit = math.log(100.0)

    image = image_tokens[0]
    corner = permute(
        image[:half, :half], lambda r, c: (r - 1) % ROWS * COLS + (c - 1) % COLS
    ).reshape(TILE, chans)
    below = permute(image[:half, half:], lambda r, c: (r - 1) % ROWS * COLS + c).reshape(
        TILE, chans
    )
    beside = permute(image[half:, :half], lambda r, c: r * COLS + (c - 1) % COLS).reshape(
        TILE, chans
    )
    corner_of = image[half:, half:].reshape(TILE, chans)
    x = jnp.concatenate([corner_of, below, beside, corner], axis=0)

    rows_four = table_rows(table_four)
    scaled_four = jnp.exp(jnp.minimum(scale_four, limit))
    swapped = [
        other_core(value)
        for value in (
            merge_weight,
            qkv_four,
            proj_four,
            expand_weight,
            reduce_weight,
            rows_four,
            scaled_four,
        )
    ]
    x, *swapped = lax.optimization_barrier((x, *swapped))
    merge_other, qkv_other, proj_other, expand_other, reduce_other = swapped[:5]
    rows_other, scaled_other = swapped[5:]

    last = jnp.stack([row == ROWS - 1, col == COLS - 1]).astype(jnp.int32)
    quadrants = first_attention(
        last,
        jnp.exp(jnp.minimum(scale_three, limit)),
        x,
        qkv_three,
        table_rows(table_three),
        proj_three,
        gain_three[None],
    )

    lower_right = permute(quadrants[0], lambda r, c: home(r, c))
    upper_right = permute(quadrants[1], lambda r, c: home(r + 1, c))
    lower_left = permute(quadrants[2], lambda r, c: home(r, c + 1))
    upper_left = permute(quadrants[3], lambda r, c: home(r + 1, c + 1))

    def beside_each_other(left, right):
        wide = left.shape[1]
        pair = [left.reshape(4, 4, wide), right.reshape(4, 4, wide)]
        return jnp.concatenate(pair, axis=1).reshape(TILE // 2, wide)

    low, high = merge(
        core[None].astype(jnp.int32),
        gather(
            beside_each_other(upper_left, upper_right), beside_each_other(lower_left, lower_right)
        ),
        merge_weight,
        merge_other,
    )

    dy = jnp.arange(GROUP, dtype=jnp.int32) // 2
    dz = jnp.arange(GROUP, dtype=jnp.int32) % 2
    far = (y - dy) % 4
    place = far // 2 * 4 + (zl ^ dz) * 2 + far % 2
    channel = (zh ^ dz) * 4 + far
    at = jnp.concatenate([place, channel]).astype(jnp.int32)
    merged, *parts = second_attention(
        at,
        jnp.concatenate([scaled_four, scaled_other]),
        gather(low, high),
        (qkv_four, qkv_other),
        (rows_four, rows_other),
        (proj_four, proj_other),
        merge_gain[None],
    )
    after = join(scatter(parts), merged, gain_attend[None])

    parts = feed_forward(
        gather(after[: TILE // 2], after[TILE // 2 :]),
        (expand_weight, expand_other),
        (reduce_weight, reduce_other),
    )
    out = join(scatter(parts), after, gain_feed[None])
    out = permute(out, unhome)
    return out.reshape(1, half, half, out.shape[1])


def solution(mesh):
    in_specs = (
        P(None, "row", "col", None),
        P(),
        P(),
        P(),
        P(),
        P(),
        P(None, "row"),
        P(),
        P(None, None, "row"),
        P("row", None),
        P("row"),
        P(None, "row"),
        P(),
        P(None, "row"),
        P("row", None),
        P(),
    )
    out_specs = P(None, "row", "col", None)
    return jax.shard_map(
        on_device, mesh=mesh, in_specs=in_specs, out_specs=out_specs, check_vma=False
    )
```

```python
import functools
import math

import jax
import jax.numpy as jnp
from jax import lax
from jax.experimental import pallas as pl
from jax.experimental.pallas import tpu as pltpu
from jax.sharding import PartitionSpec as P

HD = 32
WIN = 16
TOKENS = WIN * WIN
GROUP = 8
TILE = 64
LANES = 128

EPSILON = 1e-05
FLOOR = 1e-06

ROWS = 16
COLS = 8
VMEM = 24 * 1024 * 1024
MOST = 60 * 1024 * 1024
LOG2E = math.log2(math.e)


def place_of(row, col):
    return row // 8, row // 2 % 4, row % 2, col // 2, col % 2


def flat_of(zh, y, core, x, zl):
    return (zh * 8 + y * 2 + core) * COLS + x * 2 + zl


def permute(value, target):
    pairs = [
        (row * COLS + col, target(row, col)) for row in range(ROWS) for col in range(COLS)
    ]
    return lax.ppermute(value, ("row", "col"), pairs)


def home(row, col):
    zh, y, core, x, zl = place_of(row % ROWS, col % COLS)
    return flat_of(zh ^ zl, y // 2 * 2 + core, y % 2, x, zl)


def unhome(row, col):
    zh, y, core, x, zl = place_of(row, col)
    return flat_of(zh ^ zl, y // 2 * 2 + core, y % 2, x, zl)


MEMBERS = tuple((dy, dz) for dy in range(4) for dz in range(2))
ORDER = ((0, 0), (1, 0), (3, 0), (0, 1), (2, 0), (2, 1), (1, 1), (3, 1))


def onward(row, col, dy, dz):
    zh, y, core, x, zl = place_of(row, col)
    return flat_of(zh ^ dz, (y + dy) % 4, core, x, zl ^ dz)


def send(value, dy, dz):
    return permute(value, functools.partial(onward, dy=dy, dz=dz))


def gather(value):
    side = send(value, 0, 1)
    before, after = send(value, 1, 0), send(value, 3, 0)
    far = send(jnp.concatenate([value, side], axis=0), 2, 0)
    over = send(jnp.concatenate([before, after], axis=0), 0, 1)
    return [value, before, after, side, far, over]


def scatter(lows, highs):
    far = send(highs[1], 0, 1)
    lows = [lows[0], send(lows[1], 1, 0), send(lows[2], 2, 0), send(lows[3], 3, 0)]
    low, low_side = add_up(lows, 2)
    high, *high_far = add_up([highs[0], far], 4)
    low_side = send(low_side, 0, 1)
    high_far = [send(part, dy + 1, 0) for dy, part in enumerate(high_far)]
    return [low, low_side], [high] + high_far


def other_core(value):
    return permute(value, lambda row, col: (row ^ 1) * COLS + col)


def table_rows(table, logit, *flags):
    heads = table.shape[1]
    span = 2 * WIN - 1
    grid = jnp.transpose(16.0 * LOG2E * jax.nn.sigmoid(table)).reshape(heads, span, span)
    scaled = LOG2E * jnp.exp(jnp.minimum(logit, math.log(100.0)))
    extra = [scaled] + [jnp.full((heads,), flag, jnp.float32) for flag in flags]
    extra = jnp.pad(jnp.stack(extra, axis=1), ((0, 0), (0, 32 - len(extra))))
    grid = jnp.pad(grid, ((0, 0), (0, 1), (0, 0)))
    grid = jnp.concatenate([grid, extra[:, :, None]], axis=2).reshape(heads, 8, 4, 32)
    return jnp.transpose(grid, (0, 2, 1, 3)).reshape(heads, 4, 256)


def build_bias(rows, bias_ref):
    lane = lax.broadcasted_iota(jnp.int32, (WIN, 256), 1)
    slot = lane % 32 // 8
    lows = jnp.zeros((WIN, 256), jnp.float32)
    highs = jnp.zeros((WIN, 256), jnp.float32)
    for r in range(4):
        wide = jnp.broadcast_to(rows[r : r + 1], (WIN, 256))
        skew = pltpu.roll(wide, 256 - 15, 1, stride=1, stride_axis=0)
        low = pltpu.roll(skew, 8 * r, 1) if r else skew
        high = pltpu.roll(skew, (8 * r - 8) % 256, 1) if r != 1 else skew
        lows = jnp.where(slot == r, low, lows)
        highs = jnp.where(slot == r, high, highs)
    for c in range(WIN):
        by = (256 - (15 - c) * 8) % 256
        low = pltpu.roll(lows, by, 1) if by else lows
        high = pltpu.roll(highs, by, 1) if by else highs
        for half in range(2):
            at = (half * WIN + c) * 8
            bias_ref[at : at + 8, 0:LANES] = low[half * 8 : half * 8 + 8, 0:LANES]
            bias_ref[at : at + 8, LANES : 2 * LANES] = high[half * 8 : half * 8 + 8, 0:LANES]


def unit_heads(values):
    values = values.astype(jnp.float32)
    parts = []
    for at in range(0, values.shape[0], HD):
        part = values[at : at + HD]
        length = jnp.sqrt(jnp.sum(part * part, axis=0, keepdims=True))
        parts.append((part / jnp.maximum(length, FLOOR)).astype(jnp.bfloat16))
    return jnp.concatenate(parts, axis=0)


def head_attend(queries, keys, values, head, scaled, bias, mask):
    down = lax.broadcasted_iota(jnp.int32, queries.shape, 0) // HD
    own = jnp.where(down == head, queries, jnp.zeros_like(queries))
    scores = jnp.dot(keys, own, preferred_element_type=jnp.float32)
    scores = scores * scaled + bias
    if mask is not None:
        scores = scores + mask
    peak = jnp.max(scores, axis=0, keepdims=True)
    weights = jnp.exp2(scores - peak)
    total = jnp.sum(weights, axis=0, keepdims=True)
    out = jnp.dot(values, weights.astype(jnp.bfloat16), preferred_element_type=jnp.float32)
    return out * (1.0 / total)


def project(x, qkv):
    q, k, v = (
        jnp.dot(x, weight, preferred_element_type=jnp.float32).astype(jnp.bfloat16)
        for weight in qkv
    )
    q = unit_heads(jnp.transpose(q))
    k = jnp.transpose(unit_heads(jnp.transpose(k)))
    return q, k, jnp.transpose(v)


def attend(q, k, v, rows, bias, mask, attended):
    heads = LANES // HD
    for head in range(q.shape[0] // HD):
        at = head // heads * LANES
        build_bias(rows[head], bias.at[head % 2])
        for start in range(0, q.shape[1], TOKENS):
            window = slice(start, start + TOKENS)
            out = head_attend(
                q[at : at + LANES, window],
                k[window, at : at + LANES],
                v[head * HD : (head + 1) * HD, window],
                head % heads,
                rows[head][0:1, 31:32],
                bias[head % 2],
                mask,
            )
            attended[head * HD : (head + 1) * HD, window] = out.astype(jnp.bfloat16)


def norm(values, gain):
    centre = values - jnp.mean(values, axis=-1, keepdims=True)
    spread = jnp.mean(centre * centre, axis=-1, keepdims=True)
    return centre * lax.rsqrt(spread + EPSILON) * gain


def first_kernel(x_ref, qkv_hbm, rows_ref, proj_hbm, gain_ref, *rest):
    outs, (bias, mask, attended, mixed, qkv_ref, proj_ref, arrived) = rest[:4], rest[4:]
    block = attended.shape[0]
    heads = block // HD

    def copies(i):
        at = pl.ds(pl.multiple_of(i * block, block), block)
        return (
            pltpu.make_async_copy(qkv_hbm.at[:, :, at], qkv_ref.at[:, :, at], arrived.at[0, i]),
            pltpu.make_async_copy(proj_hbm.at[at, :], proj_ref.at[at, :], arrived.at[1, i]),
        )

    for i in range(x_ref.shape[1] // block):
        for copy in copies(i):
            copy.start()
    down = lax.broadcasted_iota(jnp.int32, (TOKENS, TOKENS), 0) // TILE
    across = lax.broadcasted_iota(jnp.int32, (TOKENS, TOKENS), 1) // TILE
    apart = jnp.where(down % 2 != across % 2, rows_ref[0][1:2, 31:32], 0.0)
    apart = apart + jnp.where(down // 2 != across // 2, rows_ref[0][2:3, 31:32], 0.0)
    mask[...] = jnp.where(apart > 0, -100.0 * LOG2E, 0.0).astype(jnp.float32)
    mixed[...] = jnp.zeros_like(mixed)
    x = x_ref[...]

    def step(i, _):
        at = pl.ds(pl.multiple_of(i * block, block), block)
        for copy in copies(i):
            copy.wait()
        q, k, v = project(x_ref[...], [qkv_ref[s, :, at] for s in range(3)])
        rows = [rows_ref[i * heads + head] for head in range(heads)]
        attend(q, k, v, rows, bias, mask[...], attended)
        mixed[...] = mixed[...] + jnp.dot(
            jnp.transpose(attended[...]), proj_ref[at, :], preferred_element_type=jnp.float32
        )
        return 0

    lax.fori_loop(0, x.shape[1] // block, step, 0)
    section = (x.astype(jnp.float32) + norm(mixed[...], gain_ref[...])).astype(jnp.bfloat16)
    at = lax.broadcasted_iota(jnp.int32, (TILE, TILE), 0)
    source = at // 4 % 4 * 16 + at // 16 % 2 * 8 + at % 4 * 2 + at // 32
    pick = (lax.broadcasted_iota(jnp.int32, (TILE, TILE), 1) == source).astype(jnp.bfloat16)
    chans = x.shape[1]
    for quadrant in range(4):
        rows = section[quadrant * TILE : (quadrant + 1) * TILE]
        moved = jnp.dot(pick, rows, preferred_element_type=jnp.float32).astype(jnp.bfloat16)
        for part in range(4):
            outs[quadrant][:, part * chans : (part + 1) * chans] = moved[
                part * 16 : (part + 1) * 16
            ]


def first_attention(x, qkv, rows, proj, gain):
    chans = x.shape[1]
    vmem = pl.BlockSpec(memory_space=pltpu.VMEM)
    anywhere = pl.BlockSpec(memory_space=pltpu.HBM)
    return pl.pallas_call(
        first_kernel,
        in_specs=[vmem, anywhere, vmem, anywhere, vmem],
        out_specs=[vmem] * 4,
        out_shape=[jax.ShapeDtypeStruct((16, 4 * chans), jnp.bfloat16)] * 4,
        scratch_shapes=[
            pltpu.VMEM((2, TOKENS, TOKENS), jnp.float32),
            pltpu.VMEM((TOKENS, TOKENS), jnp.float32),
            pltpu.VMEM((2 * LANES, TOKENS), jnp.bfloat16),
            pltpu.VMEM((TOKENS, chans), jnp.float32),
            pltpu.VMEM(qkv.shape, jnp.bfloat16),
            pltpu.VMEM(proj.shape, jnp.bfloat16),
            pltpu.SemaphoreType.DMA((2, chans // (2 * LANES))),
        ],
        compiler_params=pltpu.CompilerParams(vmem_limit_bytes=MOST),
        name="first_attention",
    )(x, qkv, rows, proj, gain)


PIECES = 6


def lay(pieces, whole):
    at = 0
    for piece in pieces:
        rows = piece.shape[0]
        whole[at : at + rows, :] = piece[...]
        at += rows


def fetch(pairs, arrived):
    copies = [
        pltpu.make_async_copy(source, target, arrived.at[i])
        for i, (source, target) in enumerate(pairs)
    ]
    for copy in copies:
        copy.start()
    return copies


def land(copies):
    for copy in copies:
        copy.wait()


def merge_kernel(core_ref, *refs):
    pieces, (own_hbm, other_hbm, out_ref, x, weight, arrived) = (
        refs[:PIECES],
        refs[PIECES:],
    )
    copies = fetch([(own_hbm, weight.at[:, :LANES]), (other_hbm, weight.at[:, LANES:])], arrived)
    lay(pieces, x)
    land(copies)
    both = jnp.dot(x[...], weight[...], preferred_element_type=jnp.float32).astype(jnp.bfloat16)
    own, other = both[:, :LANES], both[:, LANES:]
    first = core_ref[0] == 0
    out_ref[:, :LANES] = jnp.where(first, own, other)
    out_ref[:, LANES:] = jnp.where(first, other, own)


def merge(core, pieces, own, other):
    smem = pl.BlockSpec(memory_space=pltpu.SMEM)
    vmem = pl.BlockSpec(memory_space=pltpu.VMEM)
    tokens = GROUP * TILE
    return pl.pallas_call(
        merge_kernel,
        in_specs=[smem] + [vmem] * PIECES + [pl.BlockSpec(memory_space=pltpu.HBM)] * 2,
        out_specs=vmem,
        out_shape=jax.ShapeDtypeStruct((tokens, 2 * LANES), jnp.bfloat16),
        scratch_shapes=[
            pltpu.VMEM((tokens, pieces[0].shape[1]), jnp.bfloat16),
            pltpu.VMEM((own.shape[0], 2 * LANES), jnp.bfloat16),
            pltpu.SemaphoreType.DMA((2,)),
        ],
        compiler_params=pltpu.CompilerParams(vmem_limit_bytes=MOST - 3 * 1024 * 1024),
        name="merge_patches",
    )(core, *pieces, own, other)


def second_kernel(at_ref, *refs):
    parts, refs = refs[:PIECES], refs[PIECES:]
    qkv_refs, rows_refs, proj_refs, gain_ref = refs[0:2], refs[2:4], refs[4:6], refs[6]
    merged_ref, outs = refs[7], refs[8:14]
    merged, bias, attended, sums, qkv, proj, arrived = refs[14:]
    sides = (slice(0, LANES), slice(LANES, 2 * LANES))
    copies = fetch(
        [(qkv_refs[i], qkv.at[:, :, sides[i]]) for i in range(2)]
        + [(proj_refs[i], proj.at[sides[i], :]) for i in range(2)],
        arrived,
    )
    wide = 2 * LANES
    half = TILE // 2
    whole = GROUP * wide
    for dy, dz, part in ((dy, dz, part) for dy, dz in ORDER for part in range(2)):
        row = pl.multiple_of(at_ref[dy * 2 + dz] * TILE + part * half, half)
        pieces = []
        for fy, fz in MEMBERS:
            index = ORDER.index((fy, fz))
            source, start = (index, 0) if index < 4 else (2 + index // 2, index % 2)
            block = ORDER.index(((dy - fy) % 4, dz ^ fz))
            start = start * GROUP * TILE + block * TILE + part * half
            piece = parts[source][start : start + half, :]
            pieces.append(piece.astype(jnp.float32))
        mean = sum(jnp.sum(piece, axis=-1, keepdims=True) for piece in pieces) / whole
        pieces = [piece - mean for piece in pieces]
        spread = sum(jnp.sum(piece * piece, axis=-1, keepdims=True) for piece in pieces) / whole
        inverse = lax.rsqrt(spread + EPSILON)
        for i, piece in enumerate(pieces):
            col = pl.multiple_of(at_ref[GROUP + i] * wide, wide)
            values = piece * inverse * gain_ref[:, pl.ds(col, wide)]
            merged[pl.ds(row, half), pl.ds(col, wide)] = values.astype(jnp.bfloat16)
    merged_ref[...] = merged[pl.ds(pl.multiple_of(at_ref[0] * TILE, TILE), TILE), :]

    land(copies[:2])
    q, k, v = project(merged[...], [qkv[s] for s in range(3)])
    rows = [rows_refs[side][head] for side in range(2) for head in range(LANES // HD)]
    attend(q, k, v, rows, bias, None, attended)
    land(copies[2:])
    sums[...] = jnp.dot(
        jnp.transpose(attended[...]), proj[...], preferred_element_type=jnp.float32
    ).astype(jnp.bfloat16)
    for dy, dz in MEMBERS:
        place = at_ref[-dy % 4 * 2 + dz]
        values = sums[pl.ds(pl.multiple_of(place * TILE, TILE), TILE), :]
        put_part(outs, dy, dz, 0, 0, sums.shape[1], values)


def second_attention(at, parts, qkv, rows, proj, gain):
    smem = pl.BlockSpec(memory_space=pltpu.SMEM)
    vmem = pl.BlockSpec(memory_space=pltpu.VMEM)
    anywhere = pl.BlockSpec(memory_space=pltpu.HBM)
    chans = gain.shape[1]
    tokens = GROUP * TILE
    tile = jax.ShapeDtypeStruct((TILE, chans), jnp.bfloat16)
    return pl.pallas_call(
        second_kernel,
        in_specs=[smem]
        + [vmem] * PIECES
        + [anywhere] * 2
        + [vmem] * 2
        + [anywhere] * 2
        + [vmem],
        out_specs=[vmem] * 7,
        out_shape=[tile] + part_shapes(chans),
        scratch_shapes=[
            pltpu.VMEM((tokens, chans), jnp.bfloat16),
            pltpu.VMEM((2, TOKENS, TOKENS), jnp.float32),
            pltpu.VMEM((2 * LANES, tokens), jnp.bfloat16),
            pltpu.VMEM((tokens, chans), jnp.bfloat16),
            pltpu.VMEM((3, chans, 2 * LANES), jnp.bfloat16),
            pltpu.VMEM((2 * LANES, chans), jnp.bfloat16),
            pltpu.SemaphoreType.DMA((4,)),
        ],
        compiler_params=pltpu.CompilerParams(vmem_limit_bytes=MOST - 2 * 1024 * 1024),
        name="second_attention",
    )(at, *parts, *qkv, *rows, *proj, gain)


def feed_kernel(*refs):
    pieces, refs = refs[:PIECES], refs[PIECES:]
    outs, (x, hidden, expand, reduce, arrived) = refs[4:10], refs[10:]
    units = expand.shape[2]
    copies = fetch(
        [(refs[side], expand.at[side]) for side in range(2)]
        + [(refs[2 + side], reduce.at[pl.ds(side * units, units)]) for side in range(2)],
        arrived,
    )
    lay(pieces, x)
    for side in range(2):
        land(copies[side : side + 1])
        lifted = jnp.dot(x[...], expand[side][...], preferred_element_type=jnp.float32)
        values = 0.5 * lifted * (1.0 + lax.erf(lifted * math.sqrt(0.5)))
        hidden[:, side * units : (side + 1) * units] = values.astype(jnp.bfloat16)
    block = 4 * LANES
    chans = reduce.shape[1]
    land(copies[2:])
    for start in range(0, chans, block):
        cols = slice(start, start + block)
        total = jnp.dot(hidden[...], reduce[:, cols], preferred_element_type=jnp.float32)
        total = total.astype(jnp.bfloat16)
        for dy, dz in MEMBERS:
            at = ORDER.index((-dy % 4, dz)) * TILE
            put_part(outs, dy, dz, 0, start, chans, total[at : at + TILE])


def feed_forward(pieces, expand, reduce):
    chans, units = expand[0].shape
    tokens = GROUP * TILE
    vmem = pl.BlockSpec(memory_space=pltpu.VMEM)
    shapes = part_shapes(chans)
    return pl.pallas_call(
        feed_kernel,
        in_specs=[vmem] * PIECES + [pl.BlockSpec(memory_space=pltpu.HBM)] * 4,
        out_specs=[vmem] * len(shapes),
        out_shape=shapes,
        scratch_shapes=[
            pltpu.VMEM((tokens, chans), jnp.bfloat16),
            pltpu.VMEM((tokens, 2 * units), jnp.bfloat16),
            pltpu.VMEM((2, chans, units), jnp.bfloat16),
            pltpu.VMEM((2 * units, chans), jnp.bfloat16),
            pltpu.SemaphoreType.DMA((4,)),
        ],
        compiler_params=pltpu.CompilerParams(vmem_limit_bytes=VMEM),
        name="feed_forward",
    )(*pieces, *expand, *reduce)


def add_up(parts, count):
    total = sum(part.astype(jnp.float32) for part in parts).astype(jnp.bfloat16)
    return [total[i * TILE : (i + 1) * TILE] for i in range(count)]


def join_kernel(count, bases, *refs):
    lows, highs, refs = refs[: count[0]], refs[count[0] : sum(count)], refs[sum(count) :]
    base, gain_ref, outs = refs[:bases], refs[bases], refs[bases + 1 :]
    low, high = (sum(part[...].astype(jnp.float32) for part in parts) for parts in (lows, highs))
    total = norm(jnp.concatenate([low, high], axis=1), gain_ref[...])
    base = jnp.concatenate([part[...] for part in base], axis=0)
    total = (base.astype(jnp.float32) + total).astype(jnp.bfloat16)
    at = 0
    for out_ref in outs:
        rows = out_ref.shape[0]
        out_ref[...] = total[at : at + rows]
        at += rows


def join(lows, highs, base, gain, outs):
    vmem = pl.BlockSpec(memory_space=pltpu.VMEM)
    shape = jax.ShapeDtypeStruct((TILE // outs, gain.shape[1]), jnp.bfloat16)
    return pl.pallas_call(
        functools.partial(join_kernel, (len(lows), len(highs)), len(base)),
        in_specs=[vmem] * (len(lows) + len(highs) + len(base) + 1),
        out_specs=[vmem] * outs,
        out_shape=[shape] * outs,
        compiler_params=pltpu.CompilerParams(vmem_limit_bytes=VMEM),
        name="join_sums",
    )(*lows, *highs, *base, gain)


def part_shapes(chans):
    low = jax.ShapeDtypeStruct((2 * TILE, chans // 2), jnp.bfloat16)
    high = jax.ShapeDtypeStruct((4 * TILE, chans // 2), jnp.bfloat16)
    return [low] * 4 + [high] * 2


def put_part(outs, dy, dz, start, col, chans, values):
    rows, wide = values.shape
    middle = chans // 2
    if col < middle:
        at = dz * TILE + start
        low = min(wide, middle - col)
        outs[dy][at : at + rows, col : col + low] = values[:, :low]
    if col + wide > middle:
        at = dy * TILE + start
        skip = max(middle - col, 0)
        outs[4 + dz][at : at + rows, col + skip - middle : col + wide - middle] = values[:, skip:]


def on_device(
    image_tokens,
    qkv_three,
    proj_three,
    scale_three,
    table_three,
    gain_three,
    merge_weight,
    merge_gain,
    qkv_four,
    proj_four,
    scale_four,
    table_four,
    gain_attend,
    expand_weight,
    reduce_weight,
    gain_feed,
):
    chans = image_tokens.shape[3]
    half = WIN // 2
    row = lax.axis_index("row")
    col = lax.axis_index("col")
    zh, y, core, zl = row // 8, row // 2 % 4, row % 2, col % 2

    image = image_tokens[0]
    corner = permute(
        image[:half, :half], lambda r, c: (r - 1) % ROWS * COLS + (c - 1) % COLS
    ).reshape(TILE, chans)
    below = permute(image[:half, half:], lambda r, c: (r - 1) % ROWS * COLS + c).reshape(
        TILE, chans
    )
    beside = permute(image[half:, :half], lambda r, c: r * COLS + (c - 1) % COLS).reshape(
        TILE, chans
    )
    corner_of = image[half:, half:].reshape(TILE, chans)
    ends = ((row == ROWS - 1).astype(jnp.float32), (col == COLS - 1).astype(jnp.float32))
    rows_three = table_rows(table_three, scale_three, *ends)
    corner, below, beside, rows_three = lax.optimization_barrier(
        (corner, below, beside, rows_three)
    )
    x = jnp.concatenate([corner_of, below, beside, corner], axis=0)
    weights = (merge_weight, qkv_four, proj_four, expand_weight, reduce_weight)
    x, weights = lax.optimization_barrier((x, weights))
    merge_weight, qkv_four, proj_four, expand_weight, reduce_weight = weights
    swapped = [other_core(value) for value in weights]
    quadrants = first_attention(x, qkv_three, rows_three, proj_three, gain_three[None])
    quadrants, swapped, table_four = lax.optimization_barrier((quadrants, swapped, table_four))
    merge_other, qkv_other, proj_other, expand_other, reduce_other = swapped

    lower_right = permute(quadrants[0], lambda r, c: home(r, c))
    lower_left = permute(quadrants[2], lambda r, c: home(r, c + 1))
    upper_right = permute(quadrants[1], lambda r, c: home(r + 1, c))
    upper_left = permute(quadrants[3], lambda r, c: home(r + 1, c + 1))
    halves = (
        jnp.concatenate([left.reshape(4, 4, -1), right.reshape(4, 4, -1)], axis=1)
        for left, right in ((upper_left, upper_right), (lower_left, lower_right))
    )
    tile = jnp.concatenate(list(halves), axis=0).reshape(TILE, -1)
    rows_four = table_rows(table_four, scale_four)
    rows_other = other_core(rows_four)
    reduced = merge(core[None].astype(jnp.int32), gather(tile), merge_weight, merge_other)

    dy = jnp.arange(GROUP, dtype=jnp.int32) // 2
    dz = jnp.arange(GROUP, dtype=jnp.int32) % 2
    far = (y - dy) % 4
    place = far // 2 * 4 + (zl ^ dz) * 2 + far % 2
    channel = (zh ^ dz) * 4 + far
    at = jnp.concatenate([place, channel]).astype(jnp.int32)
    merged, *parts = second_attention(
        at,
        gather(reduced),
        (qkv_four, qkv_other),
        (rows_four, rows_other),
        (proj_four, proj_other),
        merge_gain[None],
    )
    after = join(*scatter(parts[:4], parts[4:]), [merged], gain_attend[None], 1)

    parts = feed_forward(
        gather(*after),
        (expand_weight, expand_other),
        (reduce_weight, reduce_other),
    )
    (out,) = join(*scatter(parts[:4], parts[4:]), after, gain_feed[None], 1)
    out = permute(out, unhome)
    return out.reshape(1, half, half, out.shape[1])


def solution(mesh):
    in_specs = (
        P(None, "row", "col", None),
        P(),
        P(),
        P(),
        P(),
        P(),
        P(None, "row"),
        P(),
        P(None, None, "row"),
        P("row", None),
        P("row"),
        P(None, "row"),
        P(),
        P(None, "row"),
        P("row", None),
        P(),
    )
    out_specs = P(None, "row", "col", None)
    return jax.shard_map(
        on_device, mesh=mesh, in_specs=in_specs, out_specs=out_specs, check_vma=False
    )
```

```python
import functools
import math

import jax
import jax.numpy as jnp
from jax import lax
from jax.experimental import pallas as pl
from jax.experimental.pallas import tpu as pltpu
from jax.sharding import PartitionSpec as P

HD = 32
WIN = 16
TOKENS = WIN * WIN
GROUP = 8
TILE = 64
LANES = 128

EPSILON = 1e-05
FLOOR = 1e-06

ROWS = 16
COLS = 8
VMEM = 24 * 1024 * 1024
MOST = 60 * 1024 * 1024
LOG2E = math.log2(math.e)


def place_of(row, col):
    return row // 8, row // 2 % 4, row % 2, col // 2, col % 2


def flat_of(zh, y, core, x, zl):
    return (zh * 8 + y * 2 + core) * COLS + x * 2 + zl


def permute(value, target):
    pairs = [
        (row * COLS + col, target(row, col)) for row in range(ROWS) for col in range(COLS)
    ]
    return lax.ppermute(value, ("row", "col"), pairs)


def home(row, col):
    zh, y, core, x, zl = place_of(row % ROWS, col % COLS)
    return flat_of(zh ^ zl, y // 2 * 2 + core, y % 2, x, zl)


def unhome(row, col):
    zh, y, core, x, zl = place_of(row, col)
    return flat_of(zh ^ zl, y // 2 * 2 + core, y % 2, x, zl)


MEMBERS = tuple((dy, dz) for dy in range(4) for dz in range(2))
ORDER = ((0, 0), (1, 0), (3, 0), (0, 1), (2, 0), (2, 1), (1, 1), (3, 1))


def onward(row, col, dy, dz):
    zh, y, core, x, zl = place_of(row, col)
    return flat_of(zh ^ dz, (y + dy) % 4, core, x, zl ^ dz)


def send(value, dy, dz):
    return permute(value, functools.partial(onward, dy=dy, dz=dz))


def gather(value, steps=False):
    side = send(value, 0, 1)
    before, after = send(value, 1, 0), send(value, 3, 0)
    if steps:
        half = value.shape[0] // 2
        far = [send(before[:half], 1, 0), send(after[half:], 3, 0)]
    else:
        far = [send(value, 2, 0)]
    over = send(jnp.concatenate([before, after], axis=0), 0, 1)
    return [value, before, after, side, *far, send(side, 2, 0), over]


def scatter(parts):
    own, ahead, behind, side, far, over = parts
    far = send(far, 2, 0)
    over = send(over, 0, 1)
    ahead = send(add(ahead, over[:TILE]), 1, 0)
    behind = send(add(behind, over[TILE:]), 3, 0)
    side = send(add(side, far[TILE:]), 0, 1)
    return [own, far, ahead, behind, side]


def add(one, other):
    return (one.astype(jnp.float32) + other.astype(jnp.float32)).astype(jnp.bfloat16)


def other_core(value):
    return permute(value, lambda row, col: (row ^ 1) * COLS + col)


def table_rows(table, logit, *flags):
    heads = table.shape[1]
    span = 2 * WIN - 1
    grid = jnp.transpose(16.0 * LOG2E * jax.nn.sigmoid(table)).reshape(heads, span, span)
    scaled = LOG2E * jnp.exp(jnp.minimum(logit, math.log(100.0)))
    extra = [scaled] + [jnp.full((heads,), flag, jnp.float32) for flag in flags]
    extra = jnp.pad(jnp.stack(extra, axis=1), ((0, 0), (0, 32 - len(extra))))
    grid = jnp.pad(grid, ((0, 0), (0, 1), (0, 0)))
    grid = jnp.concatenate([grid, extra[:, :, None]], axis=2).reshape(heads, 8, 4, 32)
    return jnp.transpose(grid, (0, 2, 1, 3)).reshape(heads, 4, 256)


def build_bias(rows, bias_ref):
    lane = lax.broadcasted_iota(jnp.int32, (WIN, 256), 1)
    slot = lane % 32 // 8
    lows = jnp.zeros((WIN, 256), jnp.float32)
    highs = jnp.zeros((WIN, 256), jnp.float32)
    for r in range(4):
        wide = jnp.broadcast_to(rows[r : r + 1], (WIN, 256))
        skew = pltpu.roll(wide, 256 - 15, 1, stride=1, stride_axis=0)
        low = pltpu.roll(skew, 8 * r, 1) if r else skew
        high = pltpu.roll(skew, (8 * r - 8) % 256, 1) if r != 1 else skew
        lows = jnp.where(slot == r, low, lows)
        highs = jnp.where(slot == r, high, highs)
    for c in range(WIN):
        by = (256 - (15 - c) * 8) % 256
        low = pltpu.roll(lows, by, 1) if by else lows
        high = pltpu.roll(highs, by, 1) if by else highs
        for half in range(2):
            at = (half * WIN + c) * 8
            bias_ref[at : at + 8, 0:LANES] = low[half * 8 : half * 8 + 8, 0:LANES]
            bias_ref[at : at + 8, LANES : 2 * LANES] = high[half * 8 : half * 8 + 8, 0:LANES]


def unit_heads(values):
    values = values.astype(jnp.float32)
    parts = []
    for at in range(0, values.shape[0], HD):
        part = values[at : at + HD]
        length = jnp.sqrt(jnp.sum(part * part, axis=0, keepdims=True))
        parts.append((part / jnp.maximum(length, FLOOR)).astype(jnp.bfloat16))
    return jnp.concatenate(parts, axis=0)


def head_attend(queries, keys, values, head, scaled, bias, mask):
    down = lax.broadcasted_iota(jnp.int32, queries.shape, 0) // HD
    own = jnp.where(down == head, queries, jnp.zeros_like(queries))
    scores = jnp.dot(keys, own, preferred_element_type=jnp.float32)
    scores = scores * scaled + bias
    if mask is not None:
        scores = scores + mask
    peak = jnp.max(scores, axis=0, keepdims=True)
    weights = jnp.exp2(scores - peak)
    total = jnp.sum(weights, axis=0, keepdims=True)
    out = jnp.dot(values, weights.astype(jnp.bfloat16), preferred_element_type=jnp.float32)
    return out * (1.0 / total)


def project(x, qkv):
    q, k, v = (
        jnp.dot(x, weight, preferred_element_type=jnp.float32).astype(jnp.bfloat16)
        for weight in qkv
    )
    q = unit_heads(jnp.transpose(q))
    k = jnp.transpose(unit_heads(jnp.transpose(k)))
    return q, k, jnp.transpose(v)


def attend(q, k, v, rows, bias, mask, attended):
    heads = LANES // HD
    for head in range(q.shape[0] // HD):
        at = head // heads * LANES
        build_bias(rows[head], bias.at[head % 2])
        for start in range(0, q.shape[1], TOKENS):
            window = slice(start, start + TOKENS)
            out = head_attend(
                q[at : at + LANES, window],
                k[window, at : at + LANES],
                v[head * HD : (head + 1) * HD, window],
                head % heads,
                rows[head][0:1, 31:32],
                bias[head % 2],
                mask,
            )
            attended[head * HD : (head + 1) * HD, window] = out.astype(jnp.bfloat16)


def norm(values, gain):
    centre = values - jnp.mean(values, axis=-1, keepdims=True)
    spread = jnp.mean(centre * centre, axis=-1, keepdims=True)
    return centre * lax.rsqrt(spread + EPSILON) * gain


def first_kernel(*refs):
    quarters, (qkv_hbm, rows_ref, proj_hbm, gain_ref, *rest) = refs[:4], refs[4:]
    outs, (x_ref, bias, mask, attended, mixed, qkv_ref, proj_ref, arrived) = rest[:4], rest[4:]
    block = attended.shape[0]
    heads = block // HD

    def copies(i):
        at = pl.ds(pl.multiple_of(i * block, block), block)
        return (
            pltpu.make_async_copy(qkv_hbm.at[:, :, at], qkv_ref.at[:, :, at], arrived.at[0, i]),
            pltpu.make_async_copy(proj_hbm.at[at, :], proj_ref.at[at, :], arrived.at[1, i]),
        )

    for i in range(x_ref.shape[1] // block):
        for copy in copies(i):
            copy.start()
    lay(quarters, x_ref)
    down = lax.broadcasted_iota(jnp.int32, (TOKENS, TOKENS), 0) // TILE
    across = lax.broadcasted_iota(jnp.int32, (TOKENS, TOKENS), 1) // TILE
    apart = jnp.where(down % 2 != across % 2, rows_ref[0][1:2, 31:32], 0.0)
    apart = apart + jnp.where(down // 2 != across // 2, rows_ref[0][2:3, 31:32], 0.0)
    mask[...] = jnp.where(apart > 0, -100.0 * LOG2E, 0.0).astype(jnp.float32)
    mixed[...] = jnp.zeros_like(mixed)
    x = x_ref[...]

    def step(i, _):
        at = pl.ds(pl.multiple_of(i * block, block), block)
        for copy in copies(i):
            copy.wait()
        q, k, v = project(x_ref[...], [qkv_ref[s, :, at] for s in range(3)])
        rows = [rows_ref[i * heads + head] for head in range(heads)]
        attend(q, k, v, rows, bias, mask[...], attended)
        mixed[...] = mixed[...] + jnp.dot(
            jnp.transpose(attended[...]), proj_ref[at, :], preferred_element_type=jnp.float32
        )
        return 0

    lax.fori_loop(0, x.shape[1] // block, step, 0)
    section = (x.astype(jnp.float32) + norm(mixed[...], gain_ref[...])).astype(jnp.bfloat16)
    at = lax.broadcasted_iota(jnp.int32, (TILE, TILE), 0)
    source = at // 4 % 4 * 16 + at // 16 % 2 * 8 + at % 4 * 2 + at // 32
    pick = (lax.broadcasted_iota(jnp.int32, (TILE, TILE), 1) == source).astype(jnp.bfloat16)
    chans = x.shape[1]
    for quadrant in range(4):
        rows = section[quadrant * TILE : (quadrant + 1) * TILE]
        moved = jnp.dot(pick, rows, preferred_element_type=jnp.float32).astype(jnp.bfloat16)
        for part in range(4):
            outs[quadrant][:, part * chans : (part + 1) * chans] = moved[
                part * 16 : (part + 1) * 16
            ]


def first_attention(quarters, qkv, rows, proj, gain):
    chans = quarters[0].shape[1]
    vmem = pl.BlockSpec(memory_space=pltpu.VMEM)
    anywhere = pl.BlockSpec(memory_space=pltpu.HBM)
    return pl.pallas_call(
        first_kernel,
        in_specs=[vmem] * 4 + [anywhere, vmem, anywhere, vmem],
        out_specs=[vmem] * 4,
        out_shape=[jax.ShapeDtypeStruct((16, 4 * chans), jnp.bfloat16)] * 4,
        scratch_shapes=[
            pltpu.VMEM((TOKENS, chans), jnp.bfloat16),
            pltpu.VMEM((2, TOKENS, TOKENS), jnp.float32),
            pltpu.VMEM((TOKENS, TOKENS), jnp.float32),
            pltpu.VMEM((2 * LANES, TOKENS), jnp.bfloat16),
            pltpu.VMEM((TOKENS, chans), jnp.float32),
            pltpu.VMEM(qkv.shape, jnp.bfloat16),
            pltpu.VMEM(proj.shape, jnp.bfloat16),
            pltpu.SemaphoreType.DMA((2, chans // (2 * LANES))),
        ],
        compiler_params=pltpu.CompilerParams(vmem_limit_bytes=MOST),
        name="first_attention",
    )(*quarters, qkv, rows, proj, gain)


PIECES = 7


def lay(pieces, whole):
    at = 0
    for piece in pieces:
        rows = piece.shape[0]
        whole[at : at + rows, :] = piece[...]
        at += rows


def rows_of(pieces, whole):
    pairs = []
    at = 0
    for piece in pieces:
        rows = piece.shape[0]
        pairs.append((piece, whole.at[at : at + rows, :]))
        at += rows
    return pairs


def fetch(pairs, arrived):
    copies = [
        pltpu.make_async_copy(source, target, arrived.at[i])
        for i, (source, target) in enumerate(pairs)
    ]
    for copy in copies:
        copy.start()
    return copies


def land(copies):
    for copy in copies:
        copy.wait()


def merge_kernel(count, core_ref, *refs):
    pieces, (own_hbm, other_hbm, out_ref, x, weight, arrived) = refs[:count], refs[count:]
    land(
        fetch(
            [(own_hbm, weight.at[:, :LANES]), (other_hbm, weight.at[:, LANES:])]
            + rows_of(pieces, x),
            arrived,
        )
    )
    both = jnp.dot(x[...], weight[...], preferred_element_type=jnp.float32).astype(jnp.bfloat16)
    own, other = both[:, :LANES], both[:, LANES:]
    first = core_ref[0] == 0
    out_ref[:, :LANES] = jnp.where(first, own, other)
    out_ref[:, LANES:] = jnp.where(first, other, own)


def merge(core, pieces, own, other):
    smem = pl.BlockSpec(memory_space=pltpu.SMEM)
    vmem = pl.BlockSpec(memory_space=pltpu.VMEM)
    tokens = GROUP * TILE
    return pl.pallas_call(
        functools.partial(merge_kernel, len(pieces)),
        in_specs=[smem] + [pl.BlockSpec(memory_space=pltpu.HBM)] * (len(pieces) + 2),
        out_specs=vmem,
        out_shape=jax.ShapeDtypeStruct((tokens, 2 * LANES), jnp.bfloat16),
        scratch_shapes=[
            pltpu.VMEM((tokens, pieces[0].shape[1]), jnp.bfloat16),
            pltpu.VMEM((own.shape[0], 2 * LANES), jnp.bfloat16),
            pltpu.SemaphoreType.DMA((len(pieces) + 2,)),
        ],
        compiler_params=pltpu.CompilerParams(vmem_limit_bytes=MOST - 3 * 1024 * 1024),
        name="merge_patches",
    )(core, *pieces, own, other)


def second_kernel(at_ref, *refs):
    parts, refs = refs[:PIECES], refs[PIECES:]
    qkv_refs, rows_refs, proj_refs, gain_ref = refs[0:2], refs[2:4], refs[4:6], refs[6]
    merged_ref, outs = refs[7], refs[8:14]
    merged, bias, attended, sums, qkv, proj, gathered, arrived = refs[14:]
    sides = (slice(0, LANES), slice(LANES, 2 * LANES))
    pieces_at = [0]
    for piece in parts[:-1]:
        pieces_at.append(pieces_at[-1] + piece.shape[0])
    copies = fetch(
        rows_of(parts, gathered)
        + [(qkv_refs[i], qkv.at[:, :, sides[i]]) for i in range(2)]
        + [(proj_refs[i], proj.at[sides[i], :]) for i in range(2)],
        arrived,
    )
    wide = 2 * LANES
    half = TILE // 2
    whole = GROUP * wide
    land(copies[:PIECES])
    copies = copies[PIECES:]
    for dy, dz, part in ((dy, dz, part) for dy, dz in ORDER for part in range(2)):
        row = pl.multiple_of(at_ref[dy * 2 + dz] * TILE + part * half, half)
        pieces = []
        for fy, fz in MEMBERS:
            index = ORDER.index((fy, fz))
            source, start = (index, 0) if index < 6 else (6, index % 2)
            block = ORDER.index(((dy - fy) % 4, dz ^ fz))
            start = start * GROUP * TILE + block * TILE + part * half
            start += pieces_at[source]
            piece = gathered[start : start + half, :]
            pieces.append(piece.astype(jnp.float32))
        mean = sum(jnp.sum(piece, axis=-1, keepdims=True) for piece in pieces) / whole
        pieces = [piece - mean for piece in pieces]
        spread = sum(jnp.sum(piece * piece, axis=-1, keepdims=True) for piece in pieces) / whole
        inverse = lax.rsqrt(spread + EPSILON)
        for i, piece in enumerate(pieces):
            col = pl.multiple_of(at_ref[GROUP + i] * wide, wide)
            values = piece * inverse * gain_ref[:, pl.ds(col, wide)]
            merged[pl.ds(row, half), pl.ds(col, wide)] = values.astype(jnp.bfloat16)
    merged_ref[...] = merged[pl.ds(pl.multiple_of(at_ref[0] * TILE, TILE), TILE), :]

    land(copies[:2])
    q, k, v = project(merged[...], [qkv[s] for s in range(3)])
    rows = [rows_refs[side][head] for side in range(2) for head in range(LANES // HD)]
    attend(q, k, v, rows, bias, None, attended)
    land(copies[2:])
    sums[...] = jnp.dot(
        jnp.transpose(attended[...]), proj[...], preferred_element_type=jnp.float32
    ).astype(jnp.bfloat16)
    for dy, dz in MEMBERS:
        place = at_ref[-dy % 4 * 2 + dz]
        values = sums[pl.ds(pl.multiple_of(place * TILE, TILE), TILE), :]
        put_part(outs, dy, dz, 0, values)


def second_attention(at, parts, qkv, rows, proj, gain):
    smem = pl.BlockSpec(memory_space=pltpu.SMEM)
    vmem = pl.BlockSpec(memory_space=pltpu.VMEM)
    anywhere = pl.BlockSpec(memory_space=pltpu.HBM)
    chans = gain.shape[1]
    tokens = GROUP * TILE
    tile = jax.ShapeDtypeStruct((TILE, chans), jnp.bfloat16)
    return pl.pallas_call(
        second_kernel,
        in_specs=[smem]
        + [anywhere] * (PIECES + 2)
        + [vmem] * 2
        + [anywhere] * 2
        + [vmem],
        out_specs=[vmem] * 7,
        out_shape=[tile] + part_shapes(chans),
        scratch_shapes=[
            pltpu.VMEM((tokens, chans), jnp.bfloat16),
            pltpu.VMEM((2, TOKENS, TOKENS), jnp.float32),
            pltpu.VMEM((2 * LANES, tokens), jnp.bfloat16),
            pltpu.VMEM((tokens, chans), jnp.bfloat16),
            pltpu.VMEM((3, chans, 2 * LANES), jnp.bfloat16),
            pltpu.VMEM((2 * LANES, chans), jnp.bfloat16),
            pltpu.VMEM((GROUP * tokens, 2 * LANES), jnp.bfloat16),
            pltpu.SemaphoreType.DMA((PIECES + 4,)),
        ],
        compiler_params=pltpu.CompilerParams(vmem_limit_bytes=MOST - 2 * 1024 * 1024),
        name="second_attention",
    )(at, *parts, *qkv, *rows, *proj, gain)


def feed_kernel(*refs):
    pieces, refs = refs[:PIECES], refs[PIECES:]
    outs, (x, hidden, expand, reduce, arrived) = refs[4:10], refs[10:]
    units = expand.shape[2]
    copies = fetch(
        [(refs[side], expand.at[side]) for side in range(2)]
        + [(refs[2 + side], reduce.at[pl.ds(side * units, units)]) for side in range(2)],
        arrived,
    )
    lay(pieces, x)
    for side in range(2):
        land(copies[side : side + 1])
        lifted = jnp.dot(x[...], expand[side][...], preferred_element_type=jnp.float32)
        values = 0.5 * lifted * (1.0 + lax.erf(lifted * math.sqrt(0.5)))
        hidden[:, side * units : (side + 1) * units] = values.astype(jnp.bfloat16)
    block = 4 * LANES
    chans = reduce.shape[1]
    land(copies[2:])
    for start in range(0, chans, block):
        cols = slice(start, start + block)
        total = jnp.dot(hidden[...], reduce[:, cols], preferred_element_type=jnp.float32)
        total = total.astype(jnp.bfloat16)
        for dy, dz in MEMBERS:
            at = ORDER.index((-dy % 4, dz)) * TILE
            put_part(outs, dy, dz, start, total[at : at + TILE])


def feed_forward(pieces, expand, reduce):
    chans, units = expand[0].shape
    tokens = GROUP * TILE
    vmem = pl.BlockSpec(memory_space=pltpu.VMEM)
    shapes = part_shapes(chans)
    return pl.pallas_call(
        feed_kernel,
        in_specs=[vmem] * PIECES + [pl.BlockSpec(memory_space=pltpu.HBM)] * 4,
        out_specs=[vmem] * len(shapes),
        out_shape=shapes,
        scratch_shapes=[
            pltpu.VMEM((tokens, chans), jnp.bfloat16),
            pltpu.VMEM((tokens, 2 * units), jnp.bfloat16),
            pltpu.VMEM((2, chans, units), jnp.bfloat16),
            pltpu.VMEM((2 * units, chans), jnp.bfloat16),
            pltpu.SemaphoreType.DMA((4,)),
        ],
        compiler_params=pltpu.CompilerParams(vmem_limit_bytes=VMEM),
        name="feed_forward",
    )(*pieces, *expand, *reduce)


def join_kernel(count, *refs):
    parts, (base_ref, gain_ref, out_ref) = refs[:count], refs[count:]
    total = sum(part[:TILE, :].astype(jnp.float32) for part in parts)
    out_ref[...] = (base_ref[...].astype(jnp.float32) + norm(total, gain_ref[...])).astype(
        jnp.bfloat16
    )


def join(parts, base, gain):
    vmem = pl.BlockSpec(memory_space=pltpu.VMEM)
    return pl.pallas_call(
        functools.partial(join_kernel, len(parts)),
        in_specs=[vmem] * (len(parts) + 2),
        out_specs=vmem,
        out_shape=jax.ShapeDtypeStruct(base.shape, jnp.bfloat16),
        compiler_params=pltpu.CompilerParams(vmem_limit_bytes=VMEM),
        name="join_sums",
    )(*parts, base, gain)


def part_shapes(chans):
    one = jax.ShapeDtypeStruct((TILE, chans), jnp.bfloat16)
    two = jax.ShapeDtypeStruct((2 * TILE, chans), jnp.bfloat16)
    return [one] * 4 + [two] * 2


def put_part(outs, dy, dz, col, values):
    index = ORDER.index((dy, dz))
    out_ref, start = (outs[index], 0) if index < 4 else (outs[2 + index // 2], index % 2 * TILE)
    out_ref[start : start + TILE, col : col + values.shape[1]] = values


def on_device(
    image_tokens,
    qkv_three,
    proj_three,
    scale_three,
    table_three,
    gain_three,
    merge_weight,
    merge_gain,
    qkv_four,
    proj_four,
    scale_four,
    table_four,
    gain_attend,
    expand_weight,
    reduce_weight,
    gain_feed,
):
    chans = image_tokens.shape[3]
    half = WIN // 2
    row = lax.axis_index("row")
    col = lax.axis_index("col")
    zh, y, core, zl = row // 8, row // 2 % 4, row % 2, col % 2

    image = image_tokens[0]
    corner = permute(
        image[:half, :half], lambda r, c: (r - 1) % ROWS * COLS + (c - 1) % COLS
    ).reshape(TILE, chans)
    below = permute(image[:half, half:], lambda r, c: (r - 1) % ROWS * COLS + c).reshape(
        TILE, chans
    )
    beside = permute(image[half:, :half], lambda r, c: r * COLS + (c - 1) % COLS).reshape(
        TILE, chans
    )
    corner_of = image[half:, half:].reshape(TILE, chans)
    ends = ((row == ROWS - 1).astype(jnp.float32), (col == COLS - 1).astype(jnp.float32))
    rows_three = table_rows(table_three, scale_three, *ends)
    corner, below, beside, rows_three = lax.optimization_barrier(
        (corner, below, beside, rows_three)
    )
    weights = (merge_weight, qkv_four, proj_four, expand_weight, reduce_weight)
    quarters = [corner_of, below, beside, corner]
    quarters, weights = lax.optimization_barrier((quarters, weights))
    merge_weight, qkv_four, proj_four, expand_weight, reduce_weight = weights
    swapped = [other_core(value) for value in weights]
    quadrants = first_attention(quarters, qkv_three, rows_three, proj_three, gain_three[None])
    quadrants, swapped, table_four = lax.optimization_barrier((quadrants, swapped, table_four))
    merge_other, qkv_other, proj_other, expand_other, reduce_other = swapped

    lower_right = permute(quadrants[0], lambda r, c: home(r, c))
    lower_left = permute(quadrants[2], lambda r, c: home(r, c + 1))
    upper_right = permute(quadrants[1], lambda r, c: home(r + 1, c))
    upper_left = permute(quadrants[3], lambda r, c: home(r + 1, c + 1))
    halves = (
        jnp.concatenate([left.reshape(4, 4, -1), right.reshape(4, 4, -1)], axis=1)
        for left, right in ((upper_left, upper_right), (lower_left, lower_right))
    )
    tile = jnp.concatenate(list(halves), axis=0).reshape(TILE, -1)
    rows_four = table_rows(table_four, scale_four)
    rows_other = other_core(rows_four)
    reduced = merge(
        core[None].astype(jnp.int32), gather(tile, steps=True), merge_weight, merge_other
    )

    dy = jnp.arange(GROUP, dtype=jnp.int32) // 2
    dz = jnp.arange(GROUP, dtype=jnp.int32) % 2
    far = (y - dy) % 4
    place = far // 2 * 4 + (zl ^ dz) * 2 + far % 2
    channel = (zh ^ dz) * 4 + far
    at = jnp.concatenate([place, channel]).astype(jnp.int32)
    merged, *parts = second_attention(
        at,
        gather(reduced),
        (qkv_four, qkv_other),
        (rows_four, rows_other),
        (proj_four, proj_other),
        merge_gain[None],
    )
    after = join(scatter(parts), merged, gain_attend[None])
    parts = feed_forward(
        gather(after), (expand_weight, expand_other), (reduce_weight, reduce_other)
    )
    out = permute(join(scatter(parts), after, gain_feed[None]), unhome)
    return out.reshape(1, half, half, out.shape[1])


def solution(mesh):
    in_specs = (
        P(None, "row", "col", None),
        P(),
        P(),
        P(),
        P(),
        P(),
        P(None, "row"),
        P(),
        P(None, None, "row"),
        P("row", None),
        P("row"),
        P(None, "row"),
        P(),
        P(None, "row"),
        P("row", None),
        P(),
    )
    out_specs = P(None, "row", "col", None)
    return jax.shard_map(
        on_device, mesh=mesh, in_specs=in_specs, out_specs=out_specs, check_vma=False
    )
```

```python
import functools
import math

import jax
import jax.numpy as jnp
from jax import lax
from jax.experimental import pallas as pl
from jax.experimental.pallas import tpu as pltpu
from jax.sharding import PartitionSpec as P

HD = 32
WIN = 16
TOKENS = WIN * WIN
GROUP = 8
TILE = 64
LANES = 128

EPSILON = 1e-05
FLOOR = 1e-06

ROWS = 16
COLS = 8
VMEM = 24 * 1024 * 1024
MOST = 61 * 1024 * 1024
LOG2E = math.log2(math.e)


def place_of(row, col):
    return row // 8, row // 2 % 4, row % 2, col // 2, col % 2


def flat_of(zh, y, core, x, zl):
    return (zh * 8 + y * 2 + core) * COLS + x * 2 + zl


def permute(value, target):
    pairs = [
        (row * COLS + col, target(row, col)) for row in range(ROWS) for col in range(COLS)
    ]
    return lax.ppermute(value, ("row", "col"), pairs)


def home(row, col):
    zh, y, core, x, zl = place_of(row % ROWS, col % COLS)
    return flat_of(zh ^ zl, y // 2 * 2 + core, y % 2, x, zl)


def unhome(row, col):
    zh, y, core, x, zl = place_of(row, col)
    return flat_of(zh ^ zl, y // 2 * 2 + core, y % 2, x, zl)


MEMBERS = tuple((dy, dz) for dy in range(4) for dz in range(2))
ORDER = ((0, 0), (1, 0), (3, 0), (0, 1), (2, 0), (2, 1), (1, 1), (3, 1))


def onward(row, col, dy, dz):
    zh, y, core, x, zl = place_of(row, col)
    return flat_of(zh ^ dz, (y + dy) % 4, core, x, zl ^ dz)


def send(value, dy, dz):
    return permute(value, functools.partial(onward, dy=dy, dz=dz))


def gather(value, steps=False):
    before, after = send(value, 1, 0), send(value, 3, 0)
    side = send(value, 0, 1)
    if steps:
        half = value.shape[0] // 2
        far = [send(before[:half], 1, 0), send(after[half:], 3, 0)]
    else:
        far = [send(value, 2, 0)]
    over = send(jnp.concatenate([before, after], axis=0), 0, 1)
    return [value, before, after, side, *far, send(side, 2, 0), over]


def scatter(parts):
    own, ahead, behind, side, far, over = parts
    far = send(far, 2, 0)
    over = send(over, 0, 1)
    ahead = send(add(ahead, over[:TILE]), 1, 0)
    behind = send(add(behind, over[TILE:]), 3, 0)
    side = send(add(side, far[TILE:]), 0, 1)
    return [own, far, ahead, behind, side]


def add(one, other):
    return (one.astype(jnp.float32) + other.astype(jnp.float32)).astype(jnp.bfloat16)


def other_core(value):
    return permute(value, lambda row, col: (row ^ 1) * COLS + col)


def table_rows(table, logit, *flags):
    heads = table.shape[1]
    span = 2 * WIN - 1
    grid = jnp.transpose(16.0 * LOG2E * jax.nn.sigmoid(table)).reshape(heads, span, span)
    scaled = LOG2E * jnp.exp(jnp.minimum(logit, math.log(100.0)))
    extra = [scaled] + [jnp.full((heads,), flag, jnp.float32) for flag in flags]
    extra = jnp.pad(jnp.stack(extra, axis=1), ((0, 0), (0, 32 - len(extra))))
    grid = jnp.pad(grid, ((0, 0), (0, 1), (0, 0)))
    grid = jnp.concatenate([grid, extra[:, :, None]], axis=2).reshape(heads, 8, 4, 32)
    return jnp.transpose(grid, (0, 2, 1, 3)).reshape(heads, 4, 256)


def build_bias(rows, bias_ref):
    lane = lax.broadcasted_iota(jnp.int32, (WIN, 256), 1)
    slot = lane % 32 // 8
    lows = jnp.zeros((WIN, 256), jnp.float32)
    highs = jnp.zeros((WIN, 256), jnp.float32)
    for r in range(4):
        wide = jnp.broadcast_to(rows[r : r + 1], (WIN, 256))
        skew = pltpu.roll(wide, 256 - 15, 1, stride=1, stride_axis=0)
        low = pltpu.roll(skew, 8 * r, 1) if r else skew
        high = pltpu.roll(skew, (8 * r - 8) % 256, 1) if r != 1 else skew
        lows = jnp.where(slot == r, low, lows)
        highs = jnp.where(slot == r, high, highs)
    for c in range(WIN):
        by = (256 - (15 - c) * 8) % 256
        low = pltpu.roll(lows, by, 1) if by else lows
        high = pltpu.roll(highs, by, 1) if by else highs
        for half in range(2):
            at = (half * WIN + c) * 8
            bias_ref[at : at + 8, 0:LANES] = low[half * 8 : half * 8 + 8, 0:LANES]
            bias_ref[at : at + 8, LANES : 2 * LANES] = high[half * 8 : half * 8 + 8, 0:LANES]


def unit_heads(values):
    values = values.astype(jnp.float32)
    parts = []
    for at in range(0, values.shape[0], HD):
        part = values[at : at + HD]
        length = jnp.sqrt(jnp.sum(part * part, axis=0, keepdims=True))
        parts.append((part / jnp.maximum(length, FLOOR)).astype(jnp.bfloat16))
    return jnp.concatenate(parts, axis=0)


def head_attend(queries, keys, values, head, scaled, bias, mask):
    down = lax.broadcasted_iota(jnp.int32, queries.shape, 0) // HD
    own = jnp.where(down == head, queries, jnp.zeros_like(queries))
    scores = jnp.dot(keys, own, preferred_element_type=jnp.float32)
    scores = scores * scaled + bias
    if mask is not None:
        scores = scores + mask
    peak = jnp.max(scores, axis=0, keepdims=True)
    weights = jnp.exp2(scores - peak)
    total = jnp.sum(weights, axis=0, keepdims=True)
    out = jnp.dot(values, weights.astype(jnp.bfloat16), preferred_element_type=jnp.float32)
    return out * (1.0 / total)


def project(x, qkv):
    q, k, v = (
        jnp.dot(x, weight, preferred_element_type=jnp.float32).astype(jnp.bfloat16)
        for weight in qkv
    )
    q = unit_heads(jnp.transpose(q))
    k = jnp.transpose(unit_heads(jnp.transpose(k)))
    return q, k, jnp.transpose(v)


def attend(q, k, v, rows, bias, mask, attended):
    heads = LANES // HD
    for head in range(q.shape[0] // HD):
        at = head // heads * LANES
        build_bias(rows[head], bias.at[head % 2])
        for start in range(0, q.shape[1], TOKENS):
            window = slice(start, start + TOKENS)
            out = head_attend(
                q[at : at + LANES, window],
                k[window, at : at + LANES],
                v[head * HD : (head + 1) * HD, window],
                head % heads,
                rows[head][0:1, 31:32],
                bias[head % 2],
                mask,
            )
            attended[head * HD : (head + 1) * HD, window] = out.astype(jnp.bfloat16)


def norm(values, gain):
    centre = values - jnp.mean(values, axis=-1, keepdims=True)
    spread = jnp.mean(centre * centre, axis=-1, keepdims=True)
    return centre * lax.rsqrt(spread + EPSILON) * gain


def first_kernel(*refs):
    quarters, (qkv_hbm, rows_ref, proj_hbm, gain_ref, *rest) = refs[:4], refs[4:]
    outs, (x_ref, bias, mask, attended, mixed, qkv_ref, proj_ref, arrived) = rest[:4], rest[4:]
    block = attended.shape[0]
    heads = block // HD

    def copies(i):
        at = pl.ds(pl.multiple_of(i * block, block), block)
        return (
            pltpu.make_async_copy(qkv_hbm.at[:, :, at], qkv_ref.at[:, :, at], arrived.at[0, i]),
            pltpu.make_async_copy(proj_hbm.at[at, :], proj_ref.at[at, :], arrived.at[1, i]),
        )

    for i in range(x_ref.shape[1] // block):
        for copy in copies(i):
            copy.start()
    lay(quarters, x_ref)
    down = lax.broadcasted_iota(jnp.int32, (TOKENS, TOKENS), 0) // TILE
    across = lax.broadcasted_iota(jnp.int32, (TOKENS, TOKENS), 1) // TILE
    apart = jnp.where(down % 2 != across % 2, rows_ref[0][1:2, 31:32], 0.0)
    apart = apart + jnp.where(down // 2 != across // 2, rows_ref[0][2:3, 31:32], 0.0)
    mask[...] = jnp.where(apart > 0, -100.0 * LOG2E, 0.0).astype(jnp.float32)
    mixed[...] = jnp.zeros_like(mixed)
    x = x_ref[...]

    def step(i, _):
        at = pl.ds(pl.multiple_of(i * block, block), block)
        for copy in copies(i):
            copy.wait()
        q, k, v = project(x_ref[...], [qkv_ref[s, :, at] for s in range(3)])
        rows = [rows_ref[i * heads + head] for head in range(heads)]
        attend(q, k, v, rows, bias, mask[...], attended)
        mixed[...] = mixed[...] + jnp.dot(
            jnp.transpose(attended[...]), proj_ref[at, :], preferred_element_type=jnp.float32
        )
        return 0

    lax.fori_loop(0, x.shape[1] // block, step, 0)
    section = (x.astype(jnp.float32) + norm(mixed[...], gain_ref[...])).astype(jnp.bfloat16)
    at = lax.broadcasted_iota(jnp.int32, (TILE, TILE), 0)
    source = at // 4 % 4 * 16 + at // 16 % 2 * 8 + at % 4 * 2 + at // 32
    pick = (lax.broadcasted_iota(jnp.int32, (TILE, TILE), 1) == source).astype(jnp.bfloat16)
    chans = x.shape[1]
    for quadrant in range(4):
        rows = section[quadrant * TILE : (quadrant + 1) * TILE]
        moved = jnp.dot(pick, rows, preferred_element_type=jnp.float32).astype(jnp.bfloat16)
        for part in range(4):
            outs[quadrant][:, part * chans : (part + 1) * chans] = moved[
                part * 16 : (part + 1) * 16
            ]


def first_attention(quarters, qkv, rows, proj, gain):
    chans = quarters[0].shape[1]
    vmem = pl.BlockSpec(memory_space=pltpu.VMEM)
    anywhere = pl.BlockSpec(memory_space=pltpu.HBM)
    return pl.pallas_call(
        first_kernel,
        in_specs=[vmem] * 4 + [anywhere, vmem, anywhere, vmem],
        out_specs=[vmem] * 4,
        out_shape=[jax.ShapeDtypeStruct((16, 4 * chans), jnp.bfloat16)] * 4,
        scratch_shapes=[
            pltpu.VMEM((TOKENS, chans), jnp.bfloat16),
            pltpu.VMEM((2, TOKENS, TOKENS), jnp.float32),
            pltpu.VMEM((TOKENS, TOKENS), jnp.float32),
            pltpu.VMEM((2 * LANES, TOKENS), jnp.bfloat16),
            pltpu.VMEM((TOKENS, chans), jnp.float32),
            pltpu.VMEM(qkv.shape, jnp.bfloat16),
            pltpu.VMEM(proj.shape, jnp.bfloat16),
            pltpu.SemaphoreType.DMA((2, chans // (2 * LANES))),
        ],
        compiler_params=pltpu.CompilerParams(vmem_limit_bytes=MOST),
        name="first_attention",
    )(*quarters, qkv, rows, proj, gain)


PIECES = 7


def lay(pieces, whole):
    at = 0
    for piece in pieces:
        rows = piece.shape[0]
        whole[at : at + rows, :] = piece[...]
        at += rows


def rows_of(pieces, whole):
    pairs = []
    at = 0
    for piece in pieces:
        rows = piece.shape[0]
        pairs.append((piece, whole.at[at : at + rows, :]))
        at += rows
    return pairs


def fetch(pairs, arrived):
    copies = [
        pltpu.make_async_copy(source, target, arrived.at[i])
        for i, (source, target) in enumerate(pairs)
    ]
    for copy in copies:
        copy.start()
    return copies


def land(copies):
    for copy in copies:
        copy.wait()


def merge_kernel(count, ahead, core_ref, *refs):
    pieces, refs = refs[:count], refs[count:]
    own_hbm, other_hbm, *done, out_ref, x, weight, arrived = refs
    land(
        fetch(
            [(own_hbm, weight.at[:, :LANES]), (other_hbm, weight.at[:, LANES:])]
            + rows_of(pieces, x),
            arrived,
        )
    )
    both = jnp.dot(x[...], weight[...], preferred_element_type=jnp.float32).astype(jnp.bfloat16)
    own, other = both[:, :LANES], both[:, LANES:]
    first = core_ref[0] == 0
    if ahead:
        out_ref[:ahead, :] = done[0][...]
    out_ref[ahead:, :LANES] = jnp.where(first, own, other)
    out_ref[ahead:, LANES:] = jnp.where(first, other, own)


def merge(core, pieces, own, other, done=()):
    smem = pl.BlockSpec(memory_space=pltpu.SMEM)
    vmem = pl.BlockSpec(memory_space=pltpu.VMEM)
    tokens = sum(piece.shape[0] for piece in pieces)
    ahead = sum(part.shape[0] for part in done)
    return pl.pallas_call(
        functools.partial(merge_kernel, len(pieces), ahead),
        in_specs=[smem]
        + [pl.BlockSpec(memory_space=pltpu.HBM)] * (len(pieces) + 2)
        + [vmem] * len(done),
        out_specs=vmem,
        out_shape=jax.ShapeDtypeStruct((ahead + tokens, 2 * LANES), jnp.bfloat16),
        scratch_shapes=[
            pltpu.VMEM((tokens, pieces[0].shape[1]), jnp.bfloat16),
            pltpu.VMEM((own.shape[0], 2 * LANES), jnp.bfloat16),
            pltpu.SemaphoreType.DMA((len(pieces) + 2,)),
        ],
        compiler_params=pltpu.CompilerParams(vmem_limit_bytes=MOST - 3 * 1024 * 1024),
        name="merge_patches",
    )(core, *pieces, own, other, *done)


def second_kernel(at_ref, *refs):
    parts, refs = refs[:PIECES], refs[PIECES:]
    qkv_refs, rows_refs, proj_refs, gain_ref = refs[0:2], refs[2:4], refs[4:6], refs[6]
    merged_ref, outs = refs[7], refs[8:14]
    merged, bias, attended, sums, qkv, proj, gathered, arrived = refs[14:]
    sides = (slice(0, LANES), slice(LANES, 2 * LANES))
    pieces_at = [0]
    for piece in parts[:-1]:
        pieces_at.append(pieces_at[-1] + piece.shape[0])
    copies = fetch(
        rows_of(parts, gathered)
        + [(qkv_refs[i], qkv.at[:, :, sides[i]]) for i in range(2)]
        + [(proj_refs[i], proj.at[sides[i], :]) for i in range(2)],
        arrived,
    )
    wide = 2 * LANES
    half = TILE // 2
    whole = GROUP * wide
    land(copies[:PIECES])
    copies = copies[PIECES:]
    for dy, dz, part in ((dy, dz, part) for dy, dz in ORDER for part in range(2)):
        row = pl.multiple_of(at_ref[dy * 2 + dz] * TILE + part * half, half)
        pieces = []
        for fy, fz in MEMBERS:
            index = ORDER.index((fy, fz))
            source, start = (index, 0) if index < 6 else (6, index % 2)
            block = ORDER.index(((dy - fy) % 4, dz ^ fz))
            start = start * GROUP * TILE + block * TILE + part * half
            start += pieces_at[source]
            piece = gathered[start : start + half, :]
            pieces.append(piece.astype(jnp.float32))
        mean = sum(jnp.sum(piece, axis=-1, keepdims=True) for piece in pieces) / whole
        pieces = [piece - mean for piece in pieces]
        spread = sum(jnp.sum(piece * piece, axis=-1, keepdims=True) for piece in pieces) / whole
        inverse = lax.rsqrt(spread + EPSILON)
        for i, piece in enumerate(pieces):
            col = pl.multiple_of(at_ref[GROUP + i] * wide, wide)
            values = piece * inverse * gain_ref[:, pl.ds(col, wide)]
            merged[pl.ds(row, half), pl.ds(col, wide)] = values.astype(jnp.bfloat16)
    merged_ref[...] = merged[pl.ds(pl.multiple_of(at_ref[0] * TILE, TILE), TILE), :]

    land(copies[:2])
    q, k, v = project(merged[...], [qkv[s] for s in range(3)])
    rows = [rows_refs[side][head] for side in range(2) for head in range(LANES // HD)]
    attend(q, k, v, rows, bias, None, attended)
    land(copies[2:])
    sums[...] = jnp.dot(
        jnp.transpose(attended[...]), proj[...], preferred_element_type=jnp.float32
    ).astype(jnp.bfloat16)
    for dy, dz in MEMBERS:
        place = at_ref[-dy % 4 * 2 + dz]
        values = sums[pl.ds(pl.multiple_of(place * TILE, TILE), TILE), :]
        put_part(outs, dy, dz, 0, values)


def second_attention(at, parts, qkv, rows, proj, gain):
    smem = pl.BlockSpec(memory_space=pltpu.SMEM)
    vmem = pl.BlockSpec(memory_space=pltpu.VMEM)
    anywhere = pl.BlockSpec(memory_space=pltpu.HBM)
    chans = gain.shape[1]
    tokens = GROUP * TILE
    tile = jax.ShapeDtypeStruct((TILE, chans), jnp.bfloat16)
    return pl.pallas_call(
        second_kernel,
        in_specs=[smem]
        + [anywhere] * (PIECES + 2)
        + [vmem] * 2
        + [anywhere] * 2
        + [vmem],
        out_specs=[vmem] * 7,
        out_shape=[tile] + part_shapes(chans),
        scratch_shapes=[
            pltpu.VMEM((tokens, chans), jnp.bfloat16),
            pltpu.VMEM((2, TOKENS, TOKENS), jnp.float32),
            pltpu.VMEM((2 * LANES, tokens), jnp.bfloat16),
            pltpu.VMEM((tokens, chans), jnp.bfloat16),
            pltpu.VMEM((3, chans, 2 * LANES), jnp.bfloat16),
            pltpu.VMEM((2 * LANES, chans), jnp.bfloat16),
            pltpu.VMEM((GROUP * tokens, 2 * LANES), jnp.bfloat16),
            pltpu.SemaphoreType.DMA((PIECES + 4,)),
        ],
        compiler_params=pltpu.CompilerParams(vmem_limit_bytes=MOST - 3 * 1024 * 1024),
        name="second_attention",
    )(at, *parts, *qkv, *rows, *proj, gain)


def feed_kernel(count, takes, *refs):
    pieces, refs = refs[:count], refs[count:]
    outs, (x, hidden, expand, reduce, arrived) = refs[4 : 4 + len(takes)], refs[4 + len(takes) :]
    units = expand.shape[2]
    copies = fetch(
        [(refs[side], expand.at[side]) for side in range(2)]
        + [(refs[2 + side], reduce.at[pl.ds(side * units, units)]) for side in range(2)],
        arrived,
    )
    lay(pieces, x)
    for side in range(2):
        land(copies[side : side + 1])
        lifted = jnp.dot(x[...], expand[side], preferred_element_type=jnp.float32)
        values = 0.5 * lifted * (1.0 + lax.erf(lifted * math.sqrt(0.5)))
        hidden[:, side * units : (side + 1) * units] = values.astype(jnp.bfloat16)
    block = 4 * LANES
    chans = reduce.shape[1]
    land(copies[2:])
    for col in range(0, chans, block):
        cols = slice(col, col + block)
        total = jnp.dot(hidden[...], reduce[:, cols], preferred_element_type=jnp.float32)
        total = total.astype(jnp.bfloat16)
        for out_ref, starts in zip(outs, takes):
            for i, start in enumerate(starts):
                out_ref[i * TILE : (i + 1) * TILE, cols] = total[start : start + TILE]


def feed_half(pieces, expand, reduce, takes):
    chans, units = expand[0].shape
    tokens = sum(piece.shape[0] for piece in pieces)
    vmem = pl.BlockSpec(memory_space=pltpu.VMEM)
    return pl.pallas_call(
        functools.partial(feed_kernel, len(pieces), takes),
        in_specs=[vmem] * len(pieces) + [pl.BlockSpec(memory_space=pltpu.HBM)] * 4,
        out_specs=[vmem] * len(takes),
        out_shape=[
            jax.ShapeDtypeStruct((TILE * len(starts), chans), jnp.bfloat16) for starts in takes
        ],
        scratch_shapes=[
            pltpu.VMEM((tokens, chans), jnp.bfloat16),
            pltpu.VMEM((tokens, 2 * units), jnp.bfloat16),
            pltpu.VMEM((2, chans, units), jnp.bfloat16),
            pltpu.VMEM((2 * units, chans), jnp.bfloat16),
            pltpu.SemaphoreType.DMA((4,)),
        ],
        compiler_params=pltpu.CompilerParams(vmem_limit_bytes=VMEM),
        name="feed_forward",
    )(*pieces, *expand, *reduce)


def feed_forward(pieces, expand, reduce):
    rows = {member: ORDER.index(member) * TILE for member in ORDER}

    def takes(group, base):
        return tuple(tuple(rows[-dy % 4, dz] - base for dy, dz in members) for members in group)

    near = takes((((0, 0),), ((1, 0),), ((3, 0),), ((0, 1),)), 0)
    far = takes((((2, 0), (2, 1)), ((1, 1), (3, 1))), 4 * TILE)
    return [
        *feed_half(pieces[:4], expand, reduce, near),
        *feed_half(pieces[4:], expand, reduce, far),
    ]


def join_kernel(count, *refs):
    parts, (base_ref, gain_ref, out_ref) = refs[:count], refs[count:]
    total = sum(part[:TILE, :].astype(jnp.float32) for part in parts)
    out_ref[...] = (base_ref[...].astype(jnp.float32) + norm(total, gain_ref[...])).astype(
        jnp.bfloat16
    )


def join(parts, base, gain):
    vmem = pl.BlockSpec(memory_space=pltpu.VMEM)
    return pl.pallas_call(
        functools.partial(join_kernel, len(parts)),
        in_specs=[vmem] * (len(parts) + 2),
        out_specs=vmem,
        out_shape=jax.ShapeDtypeStruct(base.shape, jnp.bfloat16),
        compiler_params=pltpu.CompilerParams(vmem_limit_bytes=VMEM),
        name="join_sums",
    )(*parts, base, gain)


def part_shapes(chans):
    one = jax.ShapeDtypeStruct((TILE, chans), jnp.bfloat16)
    two = jax.ShapeDtypeStruct((2 * TILE, chans), jnp.bfloat16)
    return [one] * 4 + [two] * 2


def put_part(outs, dy, dz, col, values):
    index = ORDER.index((dy, dz))
    out_ref, start = (outs[index], 0) if index < 4 else (outs[2 + index // 2], index % 2 * TILE)
    out_ref[start : start + TILE, col : col + values.shape[1]] = values


def on_device(
    image_tokens,
    qkv_three,
    proj_three,
    scale_three,
    table_three,
    gain_three,
    merge_weight,
    merge_gain,
    qkv_four,
    proj_four,
    scale_four,
    table_four,
    gain_attend,
    expand_weight,
    reduce_weight,
    gain_feed,
):
    chans = image_tokens.shape[3]
    half = WIN // 2
    row = lax.axis_index("row")
    col = lax.axis_index("col")
    zh, y, core, zl = row // 8, row // 2 % 4, row % 2, col % 2

    image = image_tokens[0]
    corner = permute(
        image[:half, :half], lambda r, c: (r - 1) % ROWS * COLS + (c - 1) % COLS
    ).reshape(TILE, chans)
    below = permute(image[:half, half:], lambda r, c: (r - 1) % ROWS * COLS + c).reshape(
        TILE, chans
    )
    beside = permute(image[half:, :half], lambda r, c: r * COLS + (c - 1) % COLS).reshape(
        TILE, chans
    )
    corner_of = image[half:, half:].reshape(TILE, chans)
    ends = ((row == ROWS - 1).astype(jnp.float32), (col == COLS - 1).astype(jnp.float32))
    rows_three = table_rows(table_three, scale_three, *ends)
    corner, below, beside, rows_three = lax.optimization_barrier(
        (corner, below, beside, rows_three)
    )
    weights = (merge_weight, qkv_four, proj_four, expand_weight, reduce_weight)
    quarters = [corner_of, below, beside, corner]
    quarters, weights = lax.optimization_barrier((quarters, weights))
    merge_weight, qkv_four, proj_four, expand_weight, reduce_weight = weights
    swapped = [other_core(value) for value in weights]
    quadrants = first_attention(quarters, qkv_three, rows_three, proj_three, gain_three[None])
    quadrants, swapped, table_four = lax.optimization_barrier((quadrants, swapped, table_four))
    merge_other, qkv_other, proj_other, expand_other, reduce_other = swapped

    lower_right = permute(quadrants[0], lambda r, c: home(r, c))
    lower_left = permute(quadrants[2], lambda r, c: home(r, c + 1))
    upper_right = permute(quadrants[1], lambda r, c: home(r + 1, c))
    upper_left = permute(quadrants[3], lambda r, c: home(r + 1, c + 1))
    halves = (
        jnp.concatenate([left.reshape(4, 4, -1), right.reshape(4, 4, -1)], axis=1)
        for left, right in ((upper_left, upper_right), (lower_left, lower_right))
    )
    tile = jnp.concatenate(list(halves), axis=0).reshape(TILE, -1)
    rows_four = table_rows(table_four, scale_four)
    rows_other = other_core(rows_four)
    pieces = gather(tile, steps=True)
    side = core[None].astype(jnp.int32)
    reduced = merge(side, pieces[:4], merge_weight, merge_other)
    reduced = merge(side, pieces[4:], merge_weight, merge_other, (reduced,))

    dy = jnp.arange(GROUP, dtype=jnp.int32) // 2
    dz = jnp.arange(GROUP, dtype=jnp.int32) % 2
    far = (y - dy) % 4
    place = far // 2 * 4 + (zl ^ dz) * 2 + far % 2
    channel = (zh ^ dz) * 4 + far
    at = jnp.concatenate([place, channel]).astype(jnp.int32)
    merged, *parts = second_attention(
        at,
        gather(reduced),
        (qkv_four, qkv_other),
        (rows_four, rows_other),
        (proj_four, proj_other),
        merge_gain[None],
    )
    after = join(scatter(parts), merged, gain_attend[None])
    parts = feed_forward(
        gather(after), (expand_weight, expand_other), (reduce_weight, reduce_other)
    )
    out = permute(join(scatter(parts), after, gain_feed[None]), unhome)
    return out.reshape(1, half, half, out.shape[1])


def solution(mesh):
    in_specs = (
        P(None, "row", "col", None),
        P(),
        P(),
        P(),
        P(),
        P(),
        P(None, "row"),
        P(),
        P(None, None, "row"),
        P("row", None),
        P("row"),
        P(None, "row"),
        P(),
        P(None, "row"),
        P("row", None),
        P(),
    )
    out_specs = P(None, "row", "col", None)
    return jax.shard_map(
        on_device, mesh=mesh, in_specs=in_specs, out_specs=out_specs, check_vma=False
    )
```

```python
import functools
import math

import jax
import jax.numpy as jnp
from jax import lax
from jax.experimental import pallas as pl
from jax.experimental.pallas import tpu as pltpu
from jax.sharding import PartitionSpec as P

HD = 32
WIN = 16
TOKENS = WIN * WIN
GROUP = 8
TILE = 64
LANES = 128

EPSILON = 1e-05
FLOOR = 1e-06

ROWS = 16
COLS = 8
VMEM = 24 * 1024 * 1024
MOST = 61 * 1024 * 1024
LOG2E = math.log2(math.e)


def place_of(row, col):
    return row // 8, row // 2 % 4, row % 2, col // 2, col % 2


def flat_of(zh, y, core, x, zl):
    return (zh * 8 + y * 2 + core) * COLS + x * 2 + zl


def permute(value, target):
    pairs = [
        (row * COLS + col, target(row, col)) for row in range(ROWS) for col in range(COLS)
    ]
    return lax.ppermute(value, ("row", "col"), pairs)


def home(row, col):
    zh, y, core, x, zl = place_of(row % ROWS, col % COLS)
    return flat_of(zh ^ zl, y // 2 * 2 + core, y % 2, x, zl)


def unhome(row, col):
    zh, y, core, x, zl = place_of(row, col)
    return flat_of(zh ^ zl, y // 2 * 2 + core, y % 2, x, zl)


MEMBERS = tuple((dy, dz) for dy in range(4) for dz in range(2))
ORDER = ((0, 0), (1, 0), (3, 0), (0, 1), (2, 0), (2, 1), (1, 1), (3, 1))


def onward(row, col, dy, dz):
    zh, y, core, x, zl = place_of(row, col)
    return flat_of(zh ^ dz, (y + dy) % 4, core, x, zl ^ dz)


def send(value, dy, dz):
    return permute(value, functools.partial(onward, dy=dy, dz=dz))


def gather(value, steps=False):
    before, after = send(value, 1, 0), send(value, 3, 0)
    side = send(value, 0, 1)
    if steps:
        half = value.shape[0] // 2
        far = [send(before[:half], 1, 0), send(after[half:], 3, 0)]
    else:
        far = [send(value, 2, 0)]
    over = send(jnp.concatenate([before, after], axis=0), 0, 1)
    return [value, before, after, side, *far, send(side, 2, 0), over]


def scatter(parts):
    own, ahead, behind, side, far, over = parts
    far = send(far, 2, 0)
    over = send(over, 0, 1)
    ahead = send(add(ahead, over[:TILE]), 1, 0)
    behind = send(add(behind, over[TILE:]), 3, 0)
    side = send(add(side, far[TILE:]), 0, 1)
    return [own, far, ahead, behind, side]


def add(one, other):
    return (one.astype(jnp.float32) + other.astype(jnp.float32)).astype(jnp.bfloat16)


def other_core(value):
    return permute(value, lambda row, col: (row ^ 1) * COLS + col)


def table_rows(table, logit, *flags):
    heads = table.shape[1]
    span = 2 * WIN - 1
    grid = jnp.transpose(16.0 * LOG2E * jax.nn.sigmoid(table)).reshape(heads, span, span)
    scaled = LOG2E * jnp.exp(jnp.minimum(logit, math.log(100.0)))
    extra = [scaled] + [jnp.full((heads,), flag, jnp.float32) for flag in flags]
    extra = jnp.pad(jnp.stack(extra, axis=1), ((0, 0), (0, 32 - len(extra))))
    grid = jnp.pad(grid, ((0, 0), (0, 1), (0, 0)))
    grid = jnp.concatenate([grid, extra[:, :, None]], axis=2).reshape(heads, 8, 4, 32)
    return jnp.transpose(grid, (0, 2, 1, 3)).reshape(heads, 4, 256)


def build_bias(rows, bias_ref):
    lane = lax.broadcasted_iota(jnp.int32, (WIN, 256), 1)
    slot = lane % 32 // 8
    lows = jnp.zeros((WIN, 256), jnp.float32)
    highs = jnp.zeros((WIN, 256), jnp.float32)
    for r in range(4):
        wide = jnp.broadcast_to(rows[r : r + 1], (WIN, 256))
        skew = pltpu.roll(wide, 256 - 15, 1, stride=1, stride_axis=0)
        low = pltpu.roll(skew, 8 * r, 1) if r else skew
        high = pltpu.roll(skew, (8 * r - 8) % 256, 1) if r != 1 else skew
        lows = jnp.where(slot == r, low, lows)
        highs = jnp.where(slot == r, high, highs)
    for c in range(WIN):
        by = (256 - (15 - c) * 8) % 256
        low = pltpu.roll(lows, by, 1) if by else lows
        high = pltpu.roll(highs, by, 1) if by else highs
        for half in range(2):
            at = (half * WIN + c) * 8
            bias_ref[at : at + 8, 0:LANES] = low[half * 8 : half * 8 + 8, 0:LANES]
            bias_ref[at : at + 8, LANES : 2 * LANES] = high[half * 8 : half * 8 + 8, 0:LANES]


def unit_heads(values):
    values = values.astype(jnp.float32)
    parts = []
    for at in range(0, values.shape[0], HD):
        part = values[at : at + HD]
        length = jnp.sqrt(jnp.sum(part * part, axis=0, keepdims=True))
        parts.append((part / jnp.maximum(length, FLOOR)).astype(jnp.bfloat16))
    return jnp.concatenate(parts, axis=0)


def head_attend(queries, keys, values, head, scaled, bias, mask):
    down = lax.broadcasted_iota(jnp.int32, queries.shape, 0) // HD
    own = jnp.where(down == head, queries, jnp.zeros_like(queries))
    scores = jnp.dot(keys, own, preferred_element_type=jnp.float32)
    scores = scores * scaled + bias
    if mask is not None:
        scores = scores + mask
    peak = jnp.max(scores, axis=0, keepdims=True)
    weights = jnp.exp2(scores - peak)
    total = jnp.sum(weights, axis=0, keepdims=True)
    out = jnp.dot(values, weights.astype(jnp.bfloat16), preferred_element_type=jnp.float32)
    return out * (1.0 / total)


def project(x, qkv):
    q, k, v = (
        jnp.dot(x, weight, preferred_element_type=jnp.float32).astype(jnp.bfloat16)
        for weight in qkv
    )
    q = unit_heads(jnp.transpose(q))
    k = jnp.transpose(unit_heads(jnp.transpose(k)))
    return q, k, jnp.transpose(v)


def attend(q, k, v, rows, bias, mask, attended):
    heads = LANES // HD
    for head in range(q.shape[0] // HD):
        at = head // heads * LANES
        build_bias(rows[head], bias.at[head % 2])
        for start in range(0, q.shape[1], TOKENS):
            window = slice(start, start + TOKENS)
            out = head_attend(
                q[at : at + LANES, window],
                k[window, at : at + LANES],
                v[head * HD : (head + 1) * HD, window],
                head % heads,
                rows[head][0:1, 31:32],
                bias[head % 2],
                mask,
            )
            attended[head * HD : (head + 1) * HD, window] = out.astype(jnp.bfloat16)


def norm(values, gain):
    centre = values - jnp.mean(values, axis=-1, keepdims=True)
    spread = jnp.mean(centre * centre, axis=-1, keepdims=True)
    return centre * lax.rsqrt(spread + EPSILON) * gain


def first_kernel(*refs):
    quarters, (qkv_hbm, rows_ref, proj_hbm, gain_ref, *rest) = refs[:4], refs[4:]
    outs, (x_ref, bias, mask, attended, mixed, qkv_ref, proj_ref, arrived) = rest[:4], rest[4:]
    block = attended.shape[0]
    heads = block // HD

    def copies(i):
        at = pl.ds(pl.multiple_of(i * block, block), block)
        return (
            pltpu.make_async_copy(qkv_hbm.at[:, :, at], qkv_ref.at[:, :, at], arrived.at[0, i]),
            pltpu.make_async_copy(proj_hbm.at[at, :], proj_ref.at[at, :], arrived.at[1, i]),
        )

    for i in range(x_ref.shape[1] // block):
        for copy in copies(i):
            copy.start()
    lay(quarters, x_ref)
    down = lax.broadcasted_iota(jnp.int32, (TOKENS, TOKENS), 0) // TILE
    across = lax.broadcasted_iota(jnp.int32, (TOKENS, TOKENS), 1) // TILE
    apart = jnp.where(down % 2 != across % 2, rows_ref[0][1:2, 31:32], 0.0)
    apart = apart + jnp.where(down // 2 != across // 2, rows_ref[0][2:3, 31:32], 0.0)
    mask[...] = jnp.where(apart > 0, -100.0 * LOG2E, 0.0).astype(jnp.float32)
    mixed[...] = jnp.zeros_like(mixed)
    x = x_ref[...]

    def step(i, _):
        at = pl.ds(pl.multiple_of(i * block, block), block)
        for copy in copies(i):
            copy.wait()
        q, k, v = project(x_ref[...], [qkv_ref[s, :, at] for s in range(3)])
        rows = [rows_ref[i * heads + head] for head in range(heads)]
        attend(q, k, v, rows, bias, mask[...], attended)
        mixed[...] = mixed[...] + jnp.dot(
            jnp.transpose(attended[...]), proj_ref[at, :], preferred_element_type=jnp.float32
        )
        return 0

    lax.fori_loop(0, x.shape[1] // block, step, 0)
    section = (x.astype(jnp.float32) + norm(mixed[...], gain_ref[...])).astype(jnp.bfloat16)
    at = lax.broadcasted_iota(jnp.int32, (TILE, TILE), 0)
    source = at // 4 % 4 * 16 + at // 16 % 2 * 8 + at % 4 * 2 + at // 32
    pick = (lax.broadcasted_iota(jnp.int32, (TILE, TILE), 1) == source).astype(jnp.bfloat16)
    chans = x.shape[1]
    for quadrant in range(4):
        rows = section[quadrant * TILE : (quadrant + 1) * TILE]
        moved = jnp.dot(pick, rows, preferred_element_type=jnp.float32).astype(jnp.bfloat16)
        for part in range(4):
            outs[quadrant][:, part * chans : (part + 1) * chans] = moved[
                part * 16 : (part + 1) * 16
            ]


def first_attention(quarters, qkv, rows, proj, gain):
    chans = quarters[0].shape[1]
    vmem = pl.BlockSpec(memory_space=pltpu.VMEM)
    anywhere = pl.BlockSpec(memory_space=pltpu.HBM)
    return pl.pallas_call(
        first_kernel,
        in_specs=[vmem] * 4 + [anywhere, vmem, anywhere, vmem],
        out_specs=[vmem] * 4,
        out_shape=[jax.ShapeDtypeStruct((16, 4 * chans), jnp.bfloat16)] * 4,
        scratch_shapes=[
            pltpu.VMEM((TOKENS, chans), jnp.bfloat16),
            pltpu.VMEM((2, TOKENS, TOKENS), jnp.float32),
            pltpu.VMEM((TOKENS, TOKENS), jnp.float32),
            pltpu.VMEM((2 * LANES, TOKENS), jnp.bfloat16),
            pltpu.VMEM((TOKENS, chans), jnp.float32),
            pltpu.VMEM(qkv.shape, jnp.bfloat16),
            pltpu.VMEM(proj.shape, jnp.bfloat16),
            pltpu.SemaphoreType.DMA((2, chans // (2 * LANES))),
        ],
        compiler_params=pltpu.CompilerParams(vmem_limit_bytes=MOST),
        name="first_attention",
    )(*quarters, qkv, rows, proj, gain)


PIECES = 7


def lay(pieces, whole):
    at = 0
    for piece in pieces:
        rows = piece.shape[0]
        whole[at : at + rows, :] = piece[...]
        at += rows


def rows_of(pieces, whole):
    pairs = []
    at = 0
    for piece in pieces:
        rows = piece.shape[0]
        pairs.append((piece, whole.at[at : at + rows, :]))
        at += rows
    return pairs


def fetch(pairs, arrived):
    copies = [
        pltpu.make_async_copy(source, target, arrived.at[i])
        for i, (source, target) in enumerate(pairs)
    ]
    for copy in copies:
        copy.start()
    return copies


def land(copies):
    for copy in copies:
        copy.wait()


def merge_kernel(count, ahead, core_ref, *refs):
    pieces, refs = refs[:count], refs[count:]
    own_hbm, other_hbm, *done, out_ref, x, weight, arrived = refs
    step = x.shape[1] // 2
    copies = []
    for i in range(2):
        cols = pl.ds(i * step, step)
        pairs = [(own_hbm.at[cols, :], weight.at[cols, :LANES])]
        pairs.append((other_hbm.at[cols, :], weight.at[cols, LANES:]))
        pairs += [(piece.at[:, cols], part.at[:, cols]) for piece, part in rows_of(pieces, x)]
        copies.append(fetch(pairs, arrived.at[i]))
    both = jnp.zeros((x.shape[0], 2 * LANES), jnp.float32)
    for i in range(2):
        cols = slice(i * step, (i + 1) * step)
        land(copies[i])
        both = both + jnp.dot(x[:, cols], weight[cols, :], preferred_element_type=jnp.float32)
    both = both.astype(jnp.bfloat16)
    own, other = both[:, :LANES], both[:, LANES:]
    first = core_ref[0] == 0
    if ahead:
        out_ref[:ahead, :] = done[0][...]
    out_ref[ahead:, :LANES] = jnp.where(first, own, other)
    out_ref[ahead:, LANES:] = jnp.where(first, other, own)


def merge(core, pieces, own, other, done=()):
    smem = pl.BlockSpec(memory_space=pltpu.SMEM)
    vmem = pl.BlockSpec(memory_space=pltpu.VMEM)
    tokens = sum(piece.shape[0] for piece in pieces)
    ahead = sum(part.shape[0] for part in done)
    return pl.pallas_call(
        functools.partial(merge_kernel, len(pieces), ahead),
        in_specs=[smem]
        + [pl.BlockSpec(memory_space=pltpu.HBM)] * (len(pieces) + 2)
        + [vmem] * len(done),
        out_specs=vmem,
        out_shape=jax.ShapeDtypeStruct((ahead + tokens, 2 * LANES), jnp.bfloat16),
        scratch_shapes=[
            pltpu.VMEM((tokens, pieces[0].shape[1]), jnp.bfloat16),
            pltpu.VMEM((own.shape[0], 2 * LANES), jnp.bfloat16),
            pltpu.SemaphoreType.DMA((2, len(pieces) + 2)),
        ],
        compiler_params=pltpu.CompilerParams(vmem_limit_bytes=MOST - 3 * 1024 * 1024),
        name="merge_patches",
    )(core, *pieces, own, other, *done)


def second_kernel(at_ref, *refs):
    parts, refs = refs[:PIECES], refs[PIECES:]
    qkv_refs, rows_refs, proj_refs, gain_ref = refs[0:2], refs[2:4], refs[4:6], refs[6]
    merged_ref, outs = refs[7], refs[8:14]
    merged, bias, attended, sums, qkv, proj, gathered, arrived = refs[14:]
    sides = (slice(0, LANES), slice(LANES, 2 * LANES))
    pieces_at = [0]
    for piece in parts[:-1]:
        pieces_at.append(pieces_at[-1] + piece.shape[0])
    copies = fetch(
        rows_of(parts, gathered)
        + [(qkv_refs[i], qkv.at[:, :, sides[i]]) for i in range(2)]
        + [(proj_refs[i], proj.at[sides[i], :]) for i in range(2)],
        arrived,
    )
    wide = 2 * LANES
    half = TILE // 2
    whole = GROUP * wide
    land(copies[:PIECES])
    copies = copies[PIECES:]
    for dy, dz, part in ((dy, dz, part) for dy, dz in ORDER for part in range(2)):
        row = pl.multiple_of(at_ref[dy * 2 + dz] * TILE + part * half, half)
        pieces = []
        for fy, fz in MEMBERS:
            index = ORDER.index((fy, fz))
            source, start = (index, 0) if index < 6 else (6, index % 2)
            block = ORDER.index(((dy - fy) % 4, dz ^ fz))
            start = start * GROUP * TILE + block * TILE + part * half
            start += pieces_at[source]
            piece = gathered[start : start + half, :]
            pieces.append(piece.astype(jnp.float32))
        mean = sum(jnp.sum(piece, axis=-1, keepdims=True) for piece in pieces) / whole
        pieces = [piece - mean for piece in pieces]
        spread = sum(jnp.sum(piece * piece, axis=-1, keepdims=True) for piece in pieces) / whole
        inverse = lax.rsqrt(spread + EPSILON)
        for i, piece in enumerate(pieces):
            col = pl.multiple_of(at_ref[GROUP + i] * wide, wide)
            values = piece * inverse * gain_ref[:, pl.ds(col, wide)]
            merged[pl.ds(row, half), pl.ds(col, wide)] = values.astype(jnp.bfloat16)
    merged_ref[...] = merged[pl.ds(pl.multiple_of(at_ref[0] * TILE, TILE), TILE), :]

    land(copies[:2])
    q, k, v = project(merged[...], [qkv[s] for s in range(3)])
    rows = [rows_refs[side][head] for side in range(2) for head in range(LANES // HD)]
    attend(q, k, v, rows, bias, None, attended)
    land(copies[2:])
    sums[...] = jnp.dot(
        jnp.transpose(attended[...]), proj[...], preferred_element_type=jnp.float32
    ).astype(jnp.bfloat16)
    for dy, dz in MEMBERS:
        place = at_ref[-dy % 4 * 2 + dz]
        values = sums[pl.ds(pl.multiple_of(place * TILE, TILE), TILE), :]
        put_part(outs, dy, dz, 0, values)


def second_attention(at, parts, qkv, rows, proj, gain):
    smem = pl.BlockSpec(memory_space=pltpu.SMEM)
    vmem = pl.BlockSpec(memory_space=pltpu.VMEM)
    anywhere = pl.BlockSpec(memory_space=pltpu.HBM)
    chans = gain.shape[1]
    tokens = GROUP * TILE
    tile = jax.ShapeDtypeStruct((TILE, chans), jnp.bfloat16)
    return pl.pallas_call(
        second_kernel,
        in_specs=[smem]
        + [anywhere] * (PIECES + 2)
        + [vmem] * 2
        + [anywhere] * 2
        + [vmem],
        out_specs=[vmem] * 7,
        out_shape=[tile] + part_shapes(chans),
        scratch_shapes=[
            pltpu.VMEM((tokens, chans), jnp.bfloat16),
            pltpu.VMEM((2, TOKENS, TOKENS), jnp.float32),
            pltpu.VMEM((2 * LANES, tokens), jnp.bfloat16),
            pltpu.VMEM((tokens, chans), jnp.bfloat16),
            pltpu.VMEM((3, chans, 2 * LANES), jnp.bfloat16),
            pltpu.VMEM((2 * LANES, chans), jnp.bfloat16),
            pltpu.VMEM((GROUP * tokens, 2 * LANES), jnp.bfloat16),
            pltpu.SemaphoreType.DMA((PIECES + 4,)),
        ],
        compiler_params=pltpu.CompilerParams(vmem_limit_bytes=MOST - 3 * 1024 * 1024),
        name="second_attention",
    )(at, *parts, *qkv, *rows, *proj, gain)


def feed_kernel(count, takes, *refs):
    pieces, refs = refs[:count], refs[count:]
    outs, (x, hidden, expand, reduce, arrived) = refs[4 : 4 + len(takes)], refs[4 + len(takes) :]
    units = expand.shape[2]
    copies = fetch(
        [(refs[side], expand.at[side]) for side in range(2)]
        + [(refs[2 + side], reduce.at[pl.ds(side * units, units)]) for side in range(2)],
        arrived,
    )
    lay(pieces, x)
    for side in range(2):
        land(copies[side : side + 1])
        lifted = jnp.dot(x[...], expand[side], preferred_element_type=jnp.float32)
        values = 0.5 * lifted * (1.0 + lax.erf(lifted * math.sqrt(0.5)))
        hidden[:, side * units : (side + 1) * units] = values.astype(jnp.bfloat16)
    block = 4 * LANES
    chans = reduce.shape[1]
    land(copies[2:])
    for col in range(0, chans, block):
        cols = slice(col, col + block)
        total = jnp.dot(hidden[...], reduce[:, cols], preferred_element_type=jnp.float32)
        total = total.astype(jnp.bfloat16)
        for out_ref, starts in zip(outs, takes):
            for i, start in enumerate(starts):
                out_ref[i * TILE : (i + 1) * TILE, cols] = total[start : start + TILE]


def feed_half(pieces, expand, reduce, takes):
    chans, units = expand[0].shape
    tokens = sum(piece.shape[0] for piece in pieces)
    vmem = pl.BlockSpec(memory_space=pltpu.VMEM)
    return pl.pallas_call(
        functools.partial(feed_kernel, len(pieces), takes),
        in_specs=[vmem] * len(pieces) + [pl.BlockSpec(memory_space=pltpu.HBM)] * 4,
        out_specs=[vmem] * len(takes),
        out_shape=[
            jax.ShapeDtypeStruct((TILE * len(starts), chans), jnp.bfloat16) for starts in takes
        ],
        scratch_shapes=[
            pltpu.VMEM((tokens, chans), jnp.bfloat16),
            pltpu.VMEM((tokens, 2 * units), jnp.bfloat16),
            pltpu.VMEM((2, chans, units), jnp.bfloat16),
            pltpu.VMEM((2 * units, chans), jnp.bfloat16),
            pltpu.SemaphoreType.DMA((4,)),
        ],
        compiler_params=pltpu.CompilerParams(vmem_limit_bytes=VMEM),
        name="feed_forward",
    )(*pieces, *expand, *reduce)


def feed_forward(pieces, expand, reduce):
    rows = {member: ORDER.index(member) * TILE for member in ORDER}

    def takes(group, base):
        return tuple(tuple(rows[-dy % 4, dz] - base for dy, dz in members) for members in group)

    near = takes((((0, 0),), ((1, 0),), ((3, 0),), ((0, 1),)), 0)
    far = takes((((2, 0), (2, 1)), ((1, 1), (3, 1))), 4 * TILE)
    return [
        *feed_half(pieces[:4], expand, reduce, near),
        *feed_half(pieces[4:], expand, reduce, far),
    ]


def join_kernel(count, *refs):
    parts, (base_ref, gain_ref, out_ref) = refs[:count], refs[count:]
    total = sum(part[:TILE, :].astype(jnp.float32) for part in parts)
    out_ref[...] = (base_ref[...].astype(jnp.float32) + norm(total, gain_ref[...])).astype(
        jnp.bfloat16
    )


def join(parts, base, gain):
    vmem = pl.BlockSpec(memory_space=pltpu.VMEM)
    return pl.pallas_call(
        functools.partial(join_kernel, len(parts)),
        in_specs=[vmem] * (len(parts) + 2),
        out_specs=vmem,
        out_shape=jax.ShapeDtypeStruct(base.shape, jnp.bfloat16),
        compiler_params=pltpu.CompilerParams(vmem_limit_bytes=VMEM),
        name="join_sums",
    )(*parts, base, gain)


def part_shapes(chans):
    one = jax.ShapeDtypeStruct((TILE, chans), jnp.bfloat16)
    two = jax.ShapeDtypeStruct((2 * TILE, chans), jnp.bfloat16)
    return [one] * 4 + [two] * 2


def put_part(outs, dy, dz, col, values):
    index = ORDER.index((dy, dz))
    out_ref, start = (outs[index], 0) if index < 4 else (outs[2 + index // 2], index % 2 * TILE)
    out_ref[start : start + TILE, col : col + values.shape[1]] = values


def on_device(
    image_tokens,
    qkv_three,
    proj_three,
    scale_three,
    table_three,
    gain_three,
    merge_weight,
    merge_gain,
    qkv_four,
    proj_four,
    scale_four,
    table_four,
    gain_attend,
    expand_weight,
    reduce_weight,
    gain_feed,
):
    chans = image_tokens.shape[3]
    half = WIN // 2
    row = lax.axis_index("row")
    col = lax.axis_index("col")
    zh, y, core, zl = row // 8, row // 2 % 4, row % 2, col % 2

    image = image_tokens[0]
    corner = permute(
        image[:half, :half], lambda r, c: (r - 1) % ROWS * COLS + (c - 1) % COLS
    ).reshape(TILE, chans)
    below = permute(image[:half, half:], lambda r, c: (r - 1) % ROWS * COLS + c).reshape(
        TILE, chans
    )
    beside = permute(image[half:, :half], lambda r, c: r * COLS + (c - 1) % COLS).reshape(
        TILE, chans
    )
    corner_of = image[half:, half:].reshape(TILE, chans)
    ends = ((row == ROWS - 1).astype(jnp.float32), (col == COLS - 1).astype(jnp.float32))
    rows_three = table_rows(table_three, scale_three, *ends)
    corner, below, beside, rows_three = lax.optimization_barrier(
        (corner, below, beside, rows_three)
    )
    weights = (merge_weight, qkv_four, proj_four, expand_weight, reduce_weight)
    quarters = [corner_of, below, beside, corner]
    quarters, weights = lax.optimization_barrier((quarters, weights))
    merge_weight, qkv_four, proj_four, expand_weight, reduce_weight = weights
    swapped = [other_core(value) for value in weights]
    quadrants = first_attention(quarters, qkv_three, rows_three, proj_three, gain_three[None])
    quadrants, swapped, table_four = lax.optimization_barrier((quadrants, swapped, table_four))
    merge_other, qkv_other, proj_other, expand_other, reduce_other = swapped

    lower_right = permute(quadrants[0], lambda r, c: home(r, c))
    lower_left = permute(quadrants[2], lambda r, c: home(r, c + 1))
    upper_right = permute(quadrants[1], lambda r, c: home(r + 1, c))
    upper_left = permute(quadrants[3], lambda r, c: home(r + 1, c + 1))
    halves = (
        jnp.concatenate([left.reshape(4, 4, -1), right.reshape(4, 4, -1)], axis=1)
        for left, right in ((upper_left, upper_right), (lower_left, lower_right))
    )
    tile = jnp.concatenate(list(halves), axis=0).reshape(TILE, -1)
    rows_four = table_rows(table_four, scale_four)
    rows_other = other_core(rows_four)
    pieces = gather(tile, steps=True)
    side = core[None].astype(jnp.int32)
    reduced = merge(side, pieces[:4], merge_weight, merge_other)
    reduced = merge(side, pieces[4:], merge_weight, merge_other, (reduced,))

    dy = jnp.arange(GROUP, dtype=jnp.int32) // 2
    dz = jnp.arange(GROUP, dtype=jnp.int32) % 2
    far = (y - dy) % 4
    place = far // 2 * 4 + (zl ^ dz) * 2 + far % 2
    channel = (zh ^ dz) * 4 + far
    at = jnp.concatenate([place, channel]).astype(jnp.int32)
    merged, *parts = second_attention(
        at,
        gather(reduced),
        (qkv_four, qkv_other),
        (rows_four, rows_other),
        (proj_four, proj_other),
        merge_gain[None],
    )
    after = join(scatter(parts), merged, gain_attend[None])
    parts = feed_forward(
        gather(after), (expand_weight, expand_other), (reduce_weight, reduce_other)
    )
    out = permute(join(scatter(parts), after, gain_feed[None]), unhome)
    return out.reshape(1, half, half, out.shape[1])


def solution(mesh):
    in_specs = (
        P(None, "row", "col", None),
        P(),
        P(),
        P(),
        P(),
        P(),
        P(None, "row"),
        P(),
        P(None, None, "row"),
        P("row", None),
        P("row"),
        P(None, "row"),
        P(),
        P(None, "row"),
        P("row", None),
        P(),
    )
    out_specs = P(None, "row", "col", None)
    return jax.shard_map(
        on_device, mesh=mesh, in_specs=in_specs, out_specs=out_specs, check_vma=False
    )
```
